32 devices in a mesh: row: 4 (over z), col: 8 (over y, x, core).
Axes of the slice: x: 2, y: 2, z: 4, core: 2. Of those that a mesh axis runs over, the one named last changes fastest.
Arguments:
- tiles: bfloat16 [4, 8, 96, 256, 256], P('row', 'col'), may hold values from 0 to 1
- tile_coord: int32 [4, 8, 96, 2], P('row', 'col'), may hold values from 0 to 15, as said below
- tile_count: int32 [4, 8], P('row', 'col'), may hold values from 0 to 96, as said below
- factors: bfloat16 [16384, 256], P(('row', 'col')), may hold values from -0.09375 to 0.09375
- owner: int32 [16384], P(('row', 'col')), may hold values from 0 to 16383, as said below
- gram_inverse: float32 [256, 256], replicated, as said below
Outputs:
- solution: float32 [16384, 256], P(('row', 'col'))
The draws below stay inside these ranges and needn't reach their ends.
Inputs may be any that keep to these rules, and one draw needn't show every extreme that they name: `tile_coord`: slots below a block's count hold distinct tile positions with r * 16 + i <= c * 8 + j; later slots are unused. Some block has all 96 slots used; blocks below the diagonal have none. `tile_count`: at most 96, reached in every draw. `owner`: A permutation of 0 to 16383; each block of 512 consecutive words has exactly 16 words whose value divided by 512 is d, for every device d. `gram_inverse`: Symmetric.
All inputs are finite; a program needn't handle non-finite values.
Results may differ from the reference program's by a relative error of at most 0.0003.
Values may be sent and summed in bfloat16 or wider, within the bound.
A program may use at most 128 MiB of HBM per device.

```python
import math
import jax
import jax.numpy as jnp
from jax import lax

K = 256
TILE = 256
TR = 16
NNZ = 96
TC = 8
V = 16384
OWN = 512
SHARE = 16
N_ROW = 4
N_COL = 8
DEVICES = 32


def tile_layout(key):
    key_noise, key_want = jax.random.split(jax.random.fold_in(key, 7))
    row_ids = jnp.arange(N_ROW, dtype=jnp.int32)[:, None, None, None]
    col_ids = jnp.arange(N_COL, dtype=jnp.int32)[None, :, None, None]
    tile_i = jnp.arange(TR, dtype=jnp.int32)[None, None, :, None]
    tile_j = jnp.arange(TC, dtype=jnp.int32)[None, None, None, :]
    allowed = row_ids * TR + tile_i <= col_ids * TC + tile_j
    allowed = allowed.reshape(N_ROW, N_COL, TR * TC)
    noise = jax.random.randint(key_noise, (N_ROW, N_COL, TR * TC), 0, 1 << 16)
    scores = noise * (TR * TC) + jnp.arange(TR * TC, dtype=jnp.int32) + jnp.where(allowed, 0, (1 << 16) * (TR * TC))
    picked = jnp.argsort(scores, axis=-1)[..., :NNZ].astype(jnp.int32)
    coords = jnp.stack([picked // TC, picked % TC], axis=-1).astype(jnp.int32)
    possible = jnp.sum(allowed.astype(jnp.int32), axis=-1)
    row_top = NNZ - NNZ * jnp.arange(N_ROW, dtype=jnp.int32)[:, None] // N_ROW
    low_end = jnp.broadcast_to(row_top // 2, (N_ROW, N_COL))
    high_end = jnp.broadcast_to(row_top + 1, (N_ROW, N_COL))
    wanted = jax.random.randint(key_want, (N_ROW, N_COL), low_end, high_end).astype(jnp.int32)
    wanted = wanted.at[0, N_COL - 1].set(NNZ)
    counts = jnp.minimum(possible, wanted).astype(jnp.int32)
    return (coords, counts)


def draw_tile_coord(key, part):
    return tile_layout(key)[0]


def draw_tile_count(key, part):
    return tile_layout(key)[1]


def draw_owner(key, part):
    key_piece, key_slot = jax.random.split(jax.random.fold_in(key, 11))
    piece_scores = jax.random.randint(key_piece, (DEVICES, OWN), 0, 1 << 20) * OWN + jnp.arange(OWN, dtype=jnp.int32)
    placing = jnp.argsort(piece_scores, axis=-1).astype(jnp.int32)
    dest_ids = placing // SHARE
    within = placing % SHARE
    piece_ids = jnp.arange(DEVICES, dtype=jnp.int32)[:, None]
    first_slot = piece_ids * SHARE + within
    slot_scores = jax.random.randint(key_slot, (DEVICES, OWN), 0, 1 << 20) * OWN + jnp.arange(OWN, dtype=jnp.int32)
    slot_perm = jnp.argsort(slot_scores, axis=-1).astype(jnp.int32)
    final_slot = slot_perm[dest_ids, first_slot]
    return (dest_ids * OWN + final_slot).reshape(V).astype(jnp.int32)


def draw_gram_inverse(key, part):
    key_diag, key_off = jax.random.split(jax.random.fold_in(key, 5))
    diag_vals = jnp.exp(jax.random.uniform(key_diag, (K,), jnp.float32, math.log(0.5), math.log(2.0)))
    noise = jax.random.normal(key_off, (K, K), jnp.float32)
    off_part = (noise + noise.T) * (0.25 / math.sqrt(K))
    return jnp.diag(diag_vals) + off_part


def level_of(stream_key, shape, shards, smallest, largest):
    gain, own = 1.0, jax.random.fold_in(stream_key, 6)
    for position, parts in shards:
        heights = jnp.exp(jax.random.uniform(jax.random.fold_in(own, position), (parts,), jnp.float32, smallest / len(shards), largest / len(shards)))
        gain = gain * jnp.repeat(heights, shape[position] // parts).reshape([-1 if axis == position else 1 for axis in range(len(shape))])
    return gain


def normal_values(own_key, dims, width, most, cuts=(), held_as=jnp.bfloat16):
    drawn = width * jax.random.normal(own_key, dims, jnp.float32)
    if cuts:
        drawn = drawn * level_of(own_key, dims, cuts, -0.22, 0.18)
    return jnp.clip(drawn, -most, most).astype(held_as)


def setup_inputs(seed: int = 0) -> dict:
    key_list = jax.random.split(jax.random.key(seed), 7)
    tiles = jnp.clip(1.0 * jax.random.uniform(key_list[0], (N_ROW, N_COL, NNZ, TILE, TILE), jnp.float32) ** level_of(key_list[0], (N_ROW, N_COL, NNZ, TILE, TILE), ((0, 4), (1, 8)), -0.2, 0.2), 0.0, 1.0).astype(jnp.bfloat16)
    tile_coord = draw_tile_coord(jax.random.fold_in(key_list[6], 71), 0)
    tile_count = draw_tile_count(jax.random.fold_in(key_list[6], 71), 0)
    factors = normal_values(key_list[3], (V, K), (V // 4) ** -0.5, 0.09375, ((0, 32),))
    owner = draw_owner(jax.random.fold_in(key_list[6], 71), 0)
    gram_inverse = draw_gram_inverse(jax.random.fold_in(key_list[6], 71), 0)
    return dict(tiles=tiles, tile_coord=tile_coord, tile_count=tile_count, factors=factors, owner=owner, gram_inverse=gram_inverse)


def add_rows(accum, start_row, term):
    width_rows = term.shape[0]
    current = lax.dynamic_slice_in_dim(accum, start_row, width_rows, 0)
    return lax.dynamic_update_slice_in_dim(accum, current + term, start_row, 0)


def reference(tiles, tile_coord, tile_count, factors, owner, gram_inverse):
    tile_dim = tiles.shape[-1]
    rank_dim = factors.shape[1]
    flat_tiles = tiles.reshape(N_ROW * N_COL, NNZ, tile_dim, tile_dim)
    flat_coords = tile_coord.reshape(N_ROW * N_COL, NNZ, 2)
    flat_counts = tile_count.reshape(N_ROW * N_COL)

    def device_step(product, device):
        row_block = device // N_COL
        col_block = device % N_COL
        dev_tiles = lax.dynamic_index_in_dim(flat_tiles, device, 0, False)
        dev_coords = lax.dynamic_index_in_dim(flat_coords, device, 0, False)

        def tile_step(slot_idx, accum):
            x_tile = lax.dynamic_index_in_dim(dev_tiles, slot_idx, 0, False)
            where_now = lax.dynamic_index_in_dim(dev_coords, slot_idx, 0, False)
            tile_p = (row_block * TR + where_now[0]).astype(jnp.int32)
            tile_q = (col_block * TC + where_now[1]).astype(jnp.int32)
            start_p = (tile_p * tile_dim).astype(jnp.int32)
            start_q = (tile_q * tile_dim).astype(jnp.int32)
            w_q = lax.dynamic_slice_in_dim(factors, start_q, tile_dim, 0)
            w_p = lax.dynamic_slice_in_dim(factors, start_p, tile_dim, 0)
            accum = add_rows(accum, start_p, jnp.dot(x_tile, w_q, preferred_element_type=jnp.float32))
            upper_mask = (tile_p < tile_q).astype(jnp.float32)
            mirrored = jnp.dot(x_tile.T, w_p, preferred_element_type=jnp.float32)
            return add_rows(accum, start_q, upper_mask * mirrored)

        return lax.fori_loop(0, flat_counts[device], tile_step, product), None

    start_sum = jnp.zeros((V, rank_dim), jnp.float32)
    product, _ = lax.scan(device_step, start_sum, jnp.arange(N_ROW * N_COL, dtype=jnp.int32))
    solved = jnp.dot(product, gram_inverse, precision=lax.Precision.HIGHEST)
    return jnp.zeros((V, rank_dim), jnp.float32).at[owner].set(solved)
```

```python
import functools

import jax
import jax.numpy as jnp
from jax import lax
from jax.experimental import pallas as pl
from jax.experimental.pallas import tpu as pltpu
from jax.sharding import PartitionSpec as P

MESH = pl.DeviceIdType.MESH
ANY = pl.BlockSpec(memory_space=pl.ANY)
VMEM = pl.BlockSpec(memory_space=pltpu.VMEM)
HIGHEST = lax.Precision.HIGHEST
MIB = 1 << 20


def remote(src, dst, send_sem, recv_sem, device):
    return pltpu.make_async_remote_copy(
        src_ref=src, dst_ref=dst, send_sem=send_sem, recv_sem=recv_sem,
        device_id=device, device_id_type=MESH,
    )


def gather_kernel(n_row, n_col, f_ref, row_ref, col_ref, row_send, fwd_send, pair_send, col_send,
                  row_recv, col_recv, local_sem, diag_sem):
    r = lax.axis_index("row")
    c = lax.axis_index("col")
    ratio = n_col // n_row
    chips = n_col // 2
    k, e = c // 2, c % 2
    partner = c + 1 - 2 * e
    used = k >= r * ratio // 2
    up = c // ratio

    barrier = pltpu.get_barrier_semaphore()
    for j in range(1, n_col):
        pl.semaphore_signal(barrier, inc=1, device_id=(r, lax.rem(c + j, n_col)), device_id_type=MESH)
    for d in range(1, n_row):
        @pl.when(r - d >= 0)
        def _(d=d):
            pl.semaphore_signal(barrier, inc=1, device_id=(r - d, r * ratio + c // n_row), device_id_type=MESH)

    @pl.when(r < up)
    def _():
        for i in range(n_row):
            pl.semaphore_signal(barrier, inc=1, device_id=(up, (c % ratio) * n_row + i), device_id_type=MESH)
    pl.semaphore_wait(barrier, n_col - 1 + r + jnp.where(r < up, n_row, 0))

    def row_copy(j):
        return remote(f_ref, row_ref.at[c], row_send.at[j], row_recv.at[c],
                      (r, 2 * lax.rem(k + j, chips) + e))

    def row_goes(j):
        return lax.rem(k + j, chips) >= r * ratio // 2

    def col_copy(d):
        return remote(f_ref, col_ref.at[c % n_row], col_send.at[d], col_recv.at[c % n_row],
                      (r - d, r * ratio + c // n_row))

    for j in range(1, chips):
        @pl.when(row_goes(j))
        def _(j=j):
            row_copy(j).start()
    for d in range(n_row - 1, 0, -1):
        @pl.when(r - d >= 0)
        def _(d=d):
            col_copy(d).start()

    def source(j):
        return 2 * lax.rem(k - j + chips, chips)

    def forward(j):
        s = source(j) + e
        return remote(row_ref.at[s], row_ref.at[s], fwd_send.at[j], row_recv.at[s], (r, partner))

    def arrival(s):
        return remote(f_ref, row_ref.at[s], row_send.at[0], row_recv.at[s], (r, partner))

    @pl.when(used)
    def _():
        own = pltpu.make_async_copy(f_ref, row_ref.at[c], local_sem)
        own.start()
        pair = remote(f_ref, row_ref.at[c], pair_send, row_recv.at[c], (r, partner))
        pair.start()
        for j in range(1, chips):
            arrival(source(j) + e).wait_recv()
            forward(j).start()
        arrival(partner).wait_recv()
        for j in range(1, chips):
            arrival(source(j) + 1 - e).wait_recv()
        own.wait()
        pair.wait_send()
        for j in range(1, chips):
            forward(j).wait_send()

    @pl.when(r == up)
    def _():
        copies = [
            pltpu.make_async_copy(row_ref.at[(c % ratio) * n_row + i], col_ref.at[i], diag_sem.at[i])
            for i in range(n_row)
        ]
        for copy in copies:
            copy.start()
        for copy in copies:
            copy.wait()

    for j in range(1, chips):
        @pl.when(row_goes(j))
        def _(j=j):
            row_copy(j).wait_send()
    for d in range(n_row - 1, 0, -1):
        @pl.when(r - d >= 0)
        def _(d=d):
            col_copy(d).wait_send()

    @pl.when(r < up)
    def _():
        for i in range(n_row):
            remote(f_ref, col_ref.at[i], col_send.at[0], col_recv.at[i], (r, partner)).wait_recv()


def encode(x):
    most = jnp.max(jnp.abs(x), axis=1, keepdims=True)
    scale = jnp.maximum(most * (1.01 / 32767.0), 1e-30).astype(jnp.bfloat16).astype(jnp.float32)
    coded = jnp.round(x * (1.0 / scale)).astype(jnp.int32).astype(jnp.int16)
    return coded, scale


def split(coded):
    v = coded.astype(jnp.int32)
    high = (v + 128) >> 8
    low = v - (high << 8)
    return (
        (high << 8).astype(jnp.float32).astype(jnp.bfloat16),
        low.astype(jnp.float32).astype(jnp.bfloat16),
    )


def tile_kernel(per_step, coord_ref, meta_ref, tiles_ref, row_ref, col_ref,
                qrow_ref, qcol_ref, srow_ref, scol_ref, row_sum, col_sum):
    step = pl.program_id(0)
    count = meta_ref[0]
    tile_dim = tiles_ref.shape[-1]

    @pl.when(step == 0)
    def _():
        row_sum[...] = jnp.zeros_like(row_sum)
        col_sum[...] = jnp.zeros_like(col_sum)

    for s in range(per_step):
        slot = step * per_step + s

        @pl.when(slot < count)
        def _(s=s, slot=slot):
            i = coord_ref[2 * slot]
            j = coord_ref[2 * slot + 1]
            tile = tiles_ref[s]
            row_sum[i] += jnp.dot(tile, col_ref[j], preferred_element_type=jnp.float32)

            @pl.when(meta_ref[1] + i < meta_ref[2] + j)
            def _():
                col_sum[j] += lax.dot_general(
                    tile, row_ref[i], (((0,), (0,)), ((), ())), preferred_element_type=jnp.float32
                )

    @pl.when(step == pl.num_programs(0) - 1)
    def _():
        eye = (lax.broadcasted_iota(jnp.int32, (tile_dim, tile_dim), 0)
               == lax.broadcasted_iota(jnp.int32, (tile_dim, tile_dim), 1))

        def code(total, coded_ref, scale_ref):
            @pl.loop(0, total.shape[0])
            def _(t):
                coded, scale = encode(total[t])
                coded_ref[t] = coded
                scale_ref[t] = jnp.sum(jnp.where(eye, scale, 0.0), axis=0, keepdims=True)

        code(row_sum, qrow_ref, srow_ref)
        code(col_sum, qcol_ref, scol_ref)


def solve_kernel(n_row, n_col, pad, tile_dim, qrow_ref, qcol_ref, srow_ref, scol_ref, owner_lane, owner_sub, ginv_ref,
                 out_ref, rq, rs, cq, cs, pick, total, qa, meta, ra, rm,
                 row_send, rsc_send, col_send, csc_send, row_recv, rsc_recv, col_recv, csc_recv,
                 a_send, m_send, a_recv, m_recv, local_sem):
    r = lax.axis_index("row")
    c = lax.axis_index("col")
    me = r * n_col + c
    devices = n_row * n_col
    ratio = n_col // n_row
    own, rank = out_ref.shape
    tpd = own // tile_dim
    packed = devices * pad
    up = c // ratio
    used = r <= up

    barrier = pltpu.get_barrier_semaphore()

    @pl.loop(1, devices)
    def _(d):
        to = lax.rem(me + d, devices)
        pl.semaphore_signal(barrier, inc=1, device_id=(to // n_col, to % n_col), device_id_type=MESH)
    pl.semaphore_wait(barrier, devices - 1)

    def row_copies(j):
        to = lax.rem(c + j, n_col)
        return (
            remote(qrow_ref.at[to], rq.at[c], row_send.at[j], row_recv.at[c], (r, to)),
            remote(srow_ref.at[pl.ds(to * tpd, tpd)], rs.at[pl.ds(c * tpd, tpd)],
                   rsc_send.at[j], rsc_recv.at[c], (r, to)),
        )

    def col_copies(i):
        to = (up, (c % ratio) * n_row + i)
        return (
            remote(qcol_ref.at[i], cq.at[r], col_send.at[i], col_recv.at[r], to),
            remote(scol_ref.at[pl.ds(i * tpd, tpd)], cs.at[pl.ds(r * tpd, tpd)],
                   csc_send.at[i], csc_recv.at[r], to),
        )

    def col_here(i):
        return (
            pltpu.make_async_copy(qcol_ref.at[i], cq.at[r], col_recv.at[r]),
            pltpu.make_async_copy(scol_ref.at[pl.ds(i * tpd, tpd)], cs.at[pl.ds(r * tpd, tpd)], csc_recv.at[r]),
        )

    def col_mine(i):
        return (r == up) & ((c % ratio) * n_row + i == c)

    row_here = (
        pltpu.make_async_copy(qrow_ref.at[c], rq.at[c], row_recv.at[c]),
        pltpu.make_async_copy(srow_ref.at[pl.ds(c * tpd, tpd)], rs.at[pl.ds(c * tpd, tpd)], rsc_recv.at[c]),
    )

    @pl.when(used)
    def _():
        for i in range(n_row):
            @pl.when(jnp.logical_not(col_mine(i)))
            def _(i=i):
                for copy in col_copies(i):
                    copy.start()

            @pl.when(col_mine(i))
            def _(i=i):
                for copy in col_here(i):
                    copy.start()
        for j in range(1, n_col):
            for copy in row_copies(j):
                copy.start()
        for copy in row_here:
            copy.start()

    ow = owner_lane[...]
    dest = ow // own
    slot = (ow - dest * own).astype(jnp.float32)
    same = (owner_sub[...] // own == dest) & (
        lax.broadcasted_iota(jnp.int32, (own, own), 0) < lax.broadcasted_iota(jnp.int32, (own, own), 1))
    place = dest * pad + jnp.sum(same.astype(jnp.int32), axis=0, keepdims=True)
    chosen = lax.broadcasted_iota(jnp.int32, (packed, own), 0) == place
    pick[...] = chosen.astype(jnp.float32)
    slot_sub = jnp.sum(jnp.where(chosen, slot, 0.0), axis=1, keepdims=True)
    total[...] = jnp.zeros_like(total)

    def add(coded_ref, scales_ref, s):
        for t in range(tpd):
            words = pl.ds(t * tile_dim, tile_dim)
            scaled = (pick[:, words] * scales_ref[s * tpd + t]).astype(jnp.bfloat16)
            high, low = split(coded_ref[s, words, :])
            total[...] += (jnp.dot(scaled, high, preferred_element_type=jnp.float32)
                           + jnp.dot(scaled, low, preferred_element_type=jnp.float32))

    def row_arrival(s):
        remote(qrow_ref.at[0], rq.at[s], row_send.at[0], row_recv.at[s], (r, s)).wait_recv()
        remote(srow_ref.at[pl.ds(0, tpd)], rs.at[pl.ds(s * tpd, tpd)], rsc_send.at[0], rsc_recv.at[s],
               (r, s)).wait_recv()

    def col_arrival(s):
        remote(qcol_ref.at[0], cq.at[s], col_send.at[0], col_recv.at[s], (s, c)).wait_recv()
        remote(scol_ref.at[pl.ds(0, tpd)], cs.at[pl.ds(s * tpd, tpd)], csc_send.at[0], csc_recv.at[s],
               (s, c)).wait_recv()

    @pl.when(used)
    def _():
        for copy in row_here:
            copy.wait()
        add(rq, rs, c)

    for d in range(n_row):
        @pl.when(r - d >= 0)
        def _(d=d):
            if d == 0:
                mine = c == (r * ratio + c // n_row)

                @pl.when(mine)
                def _():
                    for copy in col_here(c % n_row):
                        copy.wait()

                @pl.when(jnp.logical_not(mine))
                def _():
                    col_arrival(r)
            else:
                col_arrival(r - d)
            add(cq, cs, r - d)

    for j in range(1, n_col):
        s = lax.rem(c - j + n_col, n_col)

        @pl.when(s >= r * ratio)
        def _(s=s):
            row_arrival(s)
            add(rq, rs, s)

    coded, scale = encode(total[...])
    qa[...] = coded.reshape(devices, pad, rank)
    lane = lax.broadcasted_iota(jnp.int32, (packed, 128), 1)
    within = lax.broadcasted_iota(jnp.int32, (packed, 128), 0) % pad
    spread = jnp.where(lane == within, scale, 0.0) + jnp.where(lane == within + 64, slot_sub, 0.0)
    meta[...] = jnp.broadcast_to(
        jnp.sum(spread.reshape(devices, pad, 128), axis=1, keepdims=True), meta.shape)

    def out_copies(d):
        to = lax.rem(me + d, devices)
        device = (to // n_col, to % n_col)
        return (
            remote(qa.at[to], ra.at[me], a_send.at[d], a_recv.at[me], device),
            remote(meta.at[to], rm.at[me], m_send.at[d], m_recv.at[me], device),
        )

    @pl.loop(1, devices)
    def _(d):
        for copy in out_copies(d):
            copy.start()
    here = (
        pltpu.make_async_copy(qa.at[me], ra.at[me], local_sem.at[0]),
        pltpu.make_async_copy(meta.at[me], rm.at[me], local_sem.at[1]),
    )
    for copy in here:
        copy.start()
    for copy in here:
        copy.wait()

    @pl.when(used)
    def _():
        for i in range(n_row):
            @pl.when(jnp.logical_not(col_mine(i)))
            def _(i=i):
                for copy in col_copies(i):
                    copy.wait_send()
        for j in range(1, n_col):
            for copy in row_copies(j):
                copy.wait_send()

    @pl.loop(1, devices)
    def _(d):
        s = lax.rem(me - d + devices, devices)
        device = (s // n_col, s % n_col)
        remote(qa.at[0], ra.at[s], a_send.at[0], a_recv.at[s], device).wait_recv()
        remote(meta.at[0], rm.at[s], m_send.at[0], m_recv.at[s], device).wait_recv()

    got = jnp.max(rm[...], axis=1)
    take = lax.broadcasted_iota(jnp.int32, (128, packed), 0)
    at = lax.broadcasted_iota(jnp.int32, (128, packed), 1) % pad
    mine = (lax.broadcasted_iota(jnp.int32, (devices, packed), 0)
            == lax.broadcasted_iota(jnp.int32, (devices, packed), 1) // pad)

    def lanes(offset):
        full = jnp.dot(got, (take == at + offset).astype(jnp.float32), precision=HIGHEST,
                       preferred_element_type=jnp.float32)
        return jnp.sum(jnp.where(mine, full, 0.0), axis=0, keepdims=True)

    scale_lane = lanes(0)
    slot_lane = jnp.round(lanes(64)).astype(jnp.int32)
    put = jnp.where(lax.broadcasted_iota(jnp.int32, (own, packed), 0) == slot_lane, scale_lane, 0.0).astype(jnp.bfloat16)
    high, low = split(ra[...].reshape(packed, rank))
    placed = (jnp.dot(put, high, preferred_element_type=jnp.float32)
              + jnp.dot(put, low, preferred_element_type=jnp.float32))
    out_ref[...] = jnp.dot(placed, ginv_ref[...], precision=HIGHEST, preferred_element_type=jnp.float32)

    @pl.loop(1, devices)
    def _(d):
        for copy in out_copies(d):
            copy.wait_send()


def per_device(n_row, n_col, tiles, tile_coord, tile_count, factors, owner, gram_inverse):
    own, rank = factors.shape
    tile_dim = tiles.shape[-1]
    slots = tiles.shape[2]
    devices = n_row * n_col
    row_tiles = own * n_col // tile_dim
    col_tiles = own * n_row // tile_dim
    tpd = own // tile_dim
    r = lax.axis_index("row")
    c = lax.axis_index("col")
    dma = pltpu.SemaphoreType.DMA

    row_panel, col_panel = pl.pallas_call(
        functools.partial(gather_kernel, n_row, n_col),
        out_shape=(
            jax.ShapeDtypeStruct((n_col, own, rank), factors.dtype),
            jax.ShapeDtypeStruct((n_row, own, rank), factors.dtype),
        ),
        in_specs=[ANY],
        out_specs=(ANY, ANY),
        scratch_shapes=[
            dma((n_col // 2,)), dma((n_col // 2,)), dma, dma((n_row,)),
            dma((n_col,)), dma((n_row,)), dma, dma((n_row,)),
        ],
        compiler_params=pltpu.CompilerParams(collective_id=0, has_side_effects=True),
        name="gather",
    )(factors)

    per_step = 8
    steps = slots // per_step
    count = tile_count[0, 0]
    numbers = jnp.stack([count, r * row_tiles, c * col_tiles]).astype(jnp.int32)
    whole = lambda *shape: pl.BlockSpec(shape, lambda g, a, b: (0,) * len(shape))
    qrow, qcol, srow, scol = pl.pallas_call(
        functools.partial(tile_kernel, per_step),
        out_shape=(
            jax.ShapeDtypeStruct((row_tiles, tile_dim, rank), jnp.int16),
            jax.ShapeDtypeStruct((col_tiles, tile_dim, rank), jnp.int16),
            jax.ShapeDtypeStruct((row_tiles, 1, tile_dim), jnp.float32),
            jax.ShapeDtypeStruct((col_tiles, 1, tile_dim), jnp.float32),
        ),
        grid_spec=pltpu.PrefetchScalarGridSpec(
            num_scalar_prefetch=2,
            grid=(steps,),
            in_specs=[
                pl.BlockSpec(
                    (per_step, tile_dim, tile_dim),
                    lambda g, a, b: (jnp.minimum(g, jnp.maximum(b[0] - 1, 0) // per_step), 0, 0),
                ),
                whole(row_tiles, tile_dim, rank),
                whole(col_tiles, tile_dim, rank),
            ],
            out_specs=(
                whole(row_tiles, tile_dim, rank),
                whole(col_tiles, tile_dim, rank),
                whole(row_tiles, 1, tile_dim),
                whole(col_tiles, 1, tile_dim),
            ),
            scratch_shapes=[
                pltpu.VMEM((row_tiles, tile_dim, rank), jnp.float32),
                pltpu.VMEM((col_tiles, tile_dim, rank), jnp.float32),
            ],
        ),
        compiler_params=pltpu.CompilerParams(vmem_limit_bytes=40 * MIB),
        name="tile_pass",
    )(
        tile_coord.reshape(-1), numbers, tiles.reshape(slots, tile_dim, tile_dim),
        row_panel.reshape(row_tiles, tile_dim, rank), col_panel.reshape(col_tiles, tile_dim, rank),
    )

    share = own // devices
    pad = -(-share // 16) * 16
    packed = devices * pad
    return pl.pallas_call(
        functools.partial(solve_kernel, n_row, n_col, pad, tile_dim),
        out_shape=jax.ShapeDtypeStruct((own, rank), jnp.float32),
        in_specs=[ANY, ANY, ANY, ANY, VMEM, VMEM, VMEM],
        out_specs=VMEM,
        scratch_shapes=[
            pltpu.VMEM((n_col, own, rank), jnp.int16),
            pltpu.VMEM((n_col * tpd, 1, tile_dim), jnp.float32),
            pltpu.VMEM((n_row, own, rank), jnp.int16),
            pltpu.VMEM((n_row * tpd, 1, tile_dim), jnp.float32),
            pltpu.VMEM((packed, own), jnp.float32),
            pltpu.VMEM((packed, rank), jnp.float32),
            pltpu.VMEM((devices, pad, rank), jnp.int16),
            pltpu.VMEM((devices, 8, 128), jnp.float32),
            pltpu.VMEM((devices, pad, rank), jnp.int16),
            pltpu.VMEM((devices, 8, 128), jnp.float32),
            dma((n_col,)), dma((n_col,)), dma((n_row,)), dma((n_row,)),
            dma((n_col,)), dma((n_col,)), dma((n_row,)), dma((n_row,)),
            dma((devices,)), dma((devices,)), dma((devices,)), dma((devices,)), dma((2,)),
        ],
        compiler_params=pltpu.CompilerParams(
            collective_id=1, has_side_effects=True, vmem_limit_bytes=40 * MIB),
        name="solve",
    )(
        qrow.reshape(n_col, own, rank), qcol.reshape(n_row, own, rank), srow, scol,
        owner.reshape(1, own), owner.reshape(own, 1), gram_inverse,
    )


def solution(mesh):
    in_specs = (
        P("row", "col", None, None, None),
        P("row", "col", None, None),
        P("row", "col"),
        P(("row", "col"), None),
        P(("row", "col")),
        P(),
    )
    out_specs = P(("row", "col"), None)
    return jax.shard_map(
        functools.partial(per_device, mesh.shape["row"], mesh.shape["col"]),
        mesh=mesh, in_specs=in_specs, out_specs=out_specs, check_vma=False,
    )
```

```python
import functools

import jax
import jax.numpy as jnp
from jax import lax
from jax.experimental import pallas as pl
from jax.experimental.pallas import tpu as pltpu
from jax.sharding import PartitionSpec as P

MESH = pl.DeviceIdType.MESH
ANY = pl.BlockSpec(memory_space=pl.ANY)
VMEM = pl.BlockSpec(memory_space=pltpu.VMEM)
HIGHEST = lax.Precision.HIGHEST
MIB = 1 << 20


def remote(src, dst, send_sem, recv_sem, device):
    return pltpu.make_async_remote_copy(
        src_ref=src, dst_ref=dst, send_sem=send_sem, recv_sem=recv_sem,
        device_id=device, device_id_type=MESH,
    )


def gather_kernel(n_row, n_col, f_ref, row_ref, row_send, fwd_send, pair_send, col_send,
                  row_recv, col_recv, local_sem):
    r = lax.axis_index("row")
    c = lax.axis_index("col")
    ratio = n_col // n_row
    chips = n_col // 2
    k, e = c // 2, c % 2
    partner = c + 1 - 2 * e
    used = k >= r * ratio // 2
    up = c // ratio

    barrier = pltpu.get_barrier_semaphore()
    for j in range(1, n_col):
        pl.semaphore_signal(barrier, inc=1, device_id=(r, lax.rem(c + j, n_col)), device_id_type=MESH)
    for d in range(1, n_row):
        @pl.when(r - d >= 0)
        def _(d=d):
            pl.semaphore_signal(barrier, inc=1, device_id=(r - d, r * ratio + c // n_row), device_id_type=MESH)

    @pl.when(r < up)
    def _():
        for i in range(n_row):
            pl.semaphore_signal(barrier, inc=1, device_id=(up, (c % ratio) * n_row + i), device_id_type=MESH)
    pl.semaphore_wait(barrier, n_col - 1 + r + jnp.where(r < up, n_row, 0))

    def row_copy(j):
        return remote(f_ref, row_ref.at[c], row_send.at[j], row_recv.at[c],
                      (r, 2 * lax.rem(k + j, chips) + e))

    def row_goes(j):
        return lax.rem(k + j, chips) >= r * ratio // 2

    def col_copy(d):
        return remote(f_ref, row_ref.at[n_col + c % n_row], col_send.at[d], col_recv.at[c % n_row],
                      (r - d, r * ratio + c // n_row))

    for j in range(1, chips):
        @pl.when(row_goes(j))
        def _(j=j):
            row_copy(j).start()
    for d in range(n_row - 1, 0, -1):
        @pl.when(r - d >= 0)
        def _(d=d):
            col_copy(d).start()

    def source(j):
        return 2 * lax.rem(k - j + chips, chips)

    def forward(j):
        s = source(j) + e
        return remote(row_ref.at[s], row_ref.at[s], fwd_send.at[j], row_recv.at[s], (r, partner))

    def arrival(s):
        return remote(f_ref, row_ref.at[s], row_send.at[0], row_recv.at[s], (r, partner))

    @pl.when(used)
    def _():
        own = pltpu.make_async_copy(f_ref, row_ref.at[c], local_sem)
        own.start()
        pair = remote(f_ref, row_ref.at[c], pair_send, row_recv.at[c], (r, partner))
        pair.start()
        for j in range(1, chips):
            arrival(source(j) + e).wait_recv()
            forward(j).start()
        arrival(partner).wait_recv()
        for j in range(1, chips):
            arrival(source(j) + 1 - e).wait_recv()
        own.wait()
        pair.wait_send()
        for j in range(1, chips):
            forward(j).wait_send()

    for j in range(1, chips):
        @pl.when(row_goes(j))
        def _(j=j):
            row_copy(j).wait_send()
    for d in range(n_row - 1, 0, -1):
        @pl.when(r - d >= 0)
        def _(d=d):
            col_copy(d).wait_send()

    @pl.when(r < up)
    def _():
        for i in range(n_row):
            remote(f_ref, row_ref.at[n_col + i], col_send.at[0], col_recv.at[i], (r, partner)).wait_recv()


def encode(x):
    most = jnp.max(jnp.abs(x), axis=1, keepdims=True)
    scale = jnp.maximum(most * (1.01 / 32767.0), 1e-30).astype(jnp.bfloat16).astype(jnp.float32)
    coded = jnp.round(x * (1.0 / scale)).astype(jnp.int32).astype(jnp.int16)
    return coded, scale


def split(coded):
    v = coded.astype(jnp.int32)
    high = (v + 128) >> 8
    low = v - (high << 8)
    return (
        (high << 8).astype(jnp.float32).astype(jnp.bfloat16),
        low.astype(jnp.float32).astype(jnp.bfloat16),
    )


def tile_kernel(per_step, coord_ref, meta_ref, tiles_ref, panel_ref,
                qrow_ref, qcol_ref, srow_ref, scol_ref, row_sum, col_sum):
    step = pl.program_id(0)
    count = meta_ref[0]
    tile_dim = tiles_ref.shape[-1]
    row_tiles = qrow_ref.shape[0]
    col_tiles = qcol_ref.shape[0]

    @pl.when(step == 0)
    def _():
        row_sum[...] = jnp.zeros_like(row_sum)
        col_sum[...] = jnp.zeros_like(col_sum)

    @pl.when(step * per_step < count)
    def _():
        for s in range(per_step):
            slot = step * per_step + s
            live = slot < count
            i = jnp.where(live, coord_ref[2 * slot], 0)
            j = jnp.where(live, coord_ref[2 * slot + 1], 0)
            upper = live & (meta_ref[1] + i < meta_ref[2] + j)
            tile = tiles_ref[s]
            row_term = jnp.dot(tile, panel_ref[meta_ref[3] + j], preferred_element_type=jnp.float32)
            col_term = lax.dot_general(
                tile, panel_ref[i], (((0,), (0,)), ((), ())), preferred_element_type=jnp.float32)
            row_sum[jnp.where(live, i, row_tiles)] += row_term
            col_sum[jnp.where(upper, j, col_tiles)] += col_term

    @pl.when(step == pl.num_programs(0) - 1)
    def _():
        eye = (lax.broadcasted_iota(jnp.int32, (tile_dim, tile_dim), 0)
               == lax.broadcasted_iota(jnp.int32, (tile_dim, tile_dim), 1))

        def code(total, coded_ref, scale_ref):
            @pl.loop(0, coded_ref.shape[0], unroll=4)
            def _(t):
                coded, scale = encode(total[t])
                coded_ref[t] = coded
                scale_ref[t] = jnp.sum(jnp.where(eye, scale, 0.0), axis=0, keepdims=True)

        code(row_sum, qrow_ref, srow_ref)
        code(col_sum, qcol_ref, scol_ref)


def solve_kernel(n_row, n_col, pad, tile_dim, qrow_ref, qcol_ref, srow_ref, scol_ref, owner_lane, owner_sub, ginv_ref,
                 out_ref, rq, rs, cq, cs, hq, hs, pick, total, qa, meta, ra, rm,
                 row_send, rsc_send, col_send, csc_send, row_recv, rsc_recv, col_recv, csc_recv,
                 hq_send, hs_send, hq_recv, hs_recv, a_send, m_send, a_recv, m_recv, local_sem):
    r = lax.axis_index("row")
    c = lax.axis_index("col")
    me = r * n_col + c
    devices = n_row * n_col
    ratio = n_col // n_row
    own, rank = out_ref.shape
    tpd = own // tile_dim
    packed = devices * pad
    up = c // ratio
    used = r <= up

    barrier = pltpu.get_barrier_semaphore()

    @pl.loop(1, devices)
    def _(d):
        to = lax.rem(me + d, devices)
        pl.semaphore_signal(barrier, inc=1, device_id=(to // n_col, to % n_col), device_id_type=MESH)
    pl.semaphore_wait(barrier, devices - 1)

    def row_copies(j):
        to = lax.rem(c + j, n_col)
        return (
            remote(qrow_ref.at[to], rq.at[c], row_send.at[j], row_recv.at[c], (r, to)),
            remote(srow_ref.at[pl.ds(to * tpd, tpd)], rs.at[pl.ds(c * tpd, tpd)],
                   rsc_send.at[j], rsc_recv.at[c], (r, to)),
        )

    def relay_copies(i):
        to = (r, (c % ratio) * n_row + i)
        return (
            remote(qcol_ref.at[i], hq.at[up], col_send.at[i], hq_recv.at[up], to),
            remote(scol_ref.at[pl.ds(i * tpd, tpd)], hs.at[pl.ds(up * tpd, tpd)],
                   csc_send.at[i], hs_recv.at[up], to),
        )

    def relay_arrival(u):
        device = (r, ratio * u + c // n_row)
        remote(qcol_ref.at[0], hq.at[u], col_send.at[0], hq_recv.at[u], device).wait_recv()
        remote(scol_ref.at[pl.ds(0, tpd)], hs.at[pl.ds(u * tpd, tpd)], csc_send.at[0], hs_recv.at[u],
               device).wait_recv()

    def hop_copies(u):
        return (
            remote(hq.at[u], cq.at[r], hq_send.at[u], col_recv.at[r], (u, c)),
            remote(hs.at[pl.ds(u * tpd, tpd)], cs.at[pl.ds(r * tpd, tpd)], hs_send.at[u], csc_recv.at[r], (u, c)),
        )

    def hops(u):
        return (u > r) & (ratio * u + c // n_row != c)

    def col_copies(i):
        to = (up, (c % ratio) * n_row + i)
        return (
            remote(qcol_ref.at[i], cq.at[r], col_send.at[i], col_recv.at[r], to),
            remote(scol_ref.at[pl.ds(i * tpd, tpd)], cs.at[pl.ds(r * tpd, tpd)],
                   csc_send.at[i], csc_recv.at[r], to),
        )

    def col_here(i):
        return (
            pltpu.make_async_copy(qcol_ref.at[i], cq.at[r], col_recv.at[r]),
            pltpu.make_async_copy(scol_ref.at[pl.ds(i * tpd, tpd)], cs.at[pl.ds(r * tpd, tpd)], csc_recv.at[r]),
        )

    def stays(i):
        return (c % ratio) * n_row + i == c

    def col_mine(i):
        return (r == up) & stays(i)

    def col_relayed(i):
        return (r < up) & jnp.logical_not(stays(i))

    def col_direct(i):
        return (r <= up) & jnp.logical_not(col_mine(i)) & jnp.logical_not(col_relayed(i))

    row_here = (
        pltpu.make_async_copy(qrow_ref.at[c], rq.at[c], row_recv.at[c]),
        pltpu.make_async_copy(srow_ref.at[pl.ds(c * tpd, tpd)], rs.at[pl.ds(c * tpd, tpd)], rsc_recv.at[c]),
    )

    @pl.when(used)
    def _():
        for i in range(n_row):
            @pl.when(col_relayed(i))
            def _(i=i):
                for copy in relay_copies(i):
                    copy.start()

            @pl.when(col_direct(i))
            def _(i=i):
                for copy in col_copies(i):
                    copy.start()

            @pl.when(col_mine(i))
            def _(i=i):
                for copy in col_here(i):
                    copy.start()
        for j in range(1, n_col):
            for copy in row_copies(j):
                copy.start()
        for copy in row_here:
            copy.start()

    ow = owner_lane[...]
    dest = ow // own
    slot = (ow - dest * own).astype(jnp.float32)
    same = (owner_sub[...] // own == dest) & (
        lax.broadcasted_iota(jnp.int32, (own, own), 0) < lax.broadcasted_iota(jnp.int32, (own, own), 1))
    place = dest * pad + jnp.sum(same.astype(jnp.int32), axis=0, keepdims=True)
    chosen = lax.broadcasted_iota(jnp.int32, (packed, own), 0) == place
    pick[...] = chosen.astype(jnp.float32)
    slot_sub = jnp.sum(jnp.where(chosen, slot, 0.0), axis=1, keepdims=True)
    total[...] = jnp.zeros_like(total)

    for u in range(n_row - 1, 0, -1):
        @pl.when(hops(u))
        def _(u=u):
            relay_arrival(u)
            for copy in hop_copies(u):
                copy.start()

    def add(coded_ref, scales_ref, s):
        for t in range(tpd):
            words = pl.ds(t * tile_dim, tile_dim)
            scaled = (pick[:, words] * scales_ref[s * tpd + t]).astype(jnp.bfloat16)
            high, low = split(coded_ref[s, words, :])
            total[...] += (jnp.dot(scaled, high, preferred_element_type=jnp.float32)
                           + jnp.dot(scaled, low, preferred_element_type=jnp.float32))

    def row_arrival(s):
        remote(qrow_ref.at[0], rq.at[s], row_send.at[0], row_recv.at[s], (r, s)).wait_recv()
        remote(srow_ref.at[pl.ds(0, tpd)], rs.at[pl.ds(s * tpd, tpd)], rsc_send.at[0], rsc_recv.at[s],
               (r, s)).wait_recv()

    def col_arrival(s):
        remote(qcol_ref.at[0], cq.at[s], col_send.at[0], col_recv.at[s], (s, c)).wait_recv()
        remote(scol_ref.at[pl.ds(0, tpd)], cs.at[pl.ds(s * tpd, tpd)], csc_send.at[0], csc_recv.at[s],
               (s, c)).wait_recv()

    @pl.when(used)
    def _():
        for copy in row_here:
            copy.wait()
        add(rq, rs, c)

    for j in range(1, n_col):
        s = lax.rem(c - j + n_col, n_col)

        @pl.when(s >= r * ratio)
        def _(s=s):
            row_arrival(s)
            add(rq, rs, s)

    for d in range(n_row):
        @pl.when(r - d >= 0)
        def _(d=d):
            if d == 0:
                mine = c == (r * ratio + c // n_row)

                @pl.when(mine)
                def _():
                    for copy in col_here(c % n_row):
                        copy.wait()

                @pl.when(jnp.logical_not(mine))
                def _():
                    col_arrival(r)
            else:
                col_arrival(r - d)
            add(cq, cs, r - d)

    coded, scale = encode(total[...])
    qa[...] = coded.reshape(devices, pad, rank)
    lane = lax.broadcasted_iota(jnp.int32, (packed, 128), 1)
    within = lax.broadcasted_iota(jnp.int32, (packed, 128), 0) % pad
    spread = jnp.where(lane == within, scale, 0.0) + jnp.where(lane == within + 64, slot_sub, 0.0)
    meta[...] = jnp.broadcast_to(
        jnp.sum(spread.reshape(devices, pad, 128), axis=1, keepdims=True), meta.shape)

    def out_copies(d):
        to = lax.rem(me + d, devices)
        device = (to // n_col, to % n_col)
        return (
            remote(qa.at[to], ra.at[me], a_send.at[d], a_recv.at[me], device),
            remote(meta.at[to], rm.at[me], m_send.at[d], m_recv.at[me], device),
        )

    @pl.loop(1, devices)
    def _(d):
        for copy in out_copies(d):
            copy.start()
    here = (
        pltpu.make_async_copy(qa.at[me], ra.at[me], local_sem.at[0]),
        pltpu.make_async_copy(meta.at[me], rm.at[me], local_sem.at[1]),
    )
    for copy in here:
        copy.start()
    for copy in here:
        copy.wait()

    @pl.when(used)
    def _():
        for i in range(n_row):
            @pl.when(col_relayed(i))
            def _(i=i):
                for copy in relay_copies(i):
                    copy.wait_send()

            @pl.when(col_direct(i))
            def _(i=i):
                for copy in col_copies(i):
                    copy.wait_send()
        for j in range(1, n_col):
            for copy in row_copies(j):
                copy.wait_send()

    for u in range(n_row - 1, 0, -1):
        @pl.when(hops(u))
        def _(u=u):
            for copy in hop_copies(u):
                copy.wait_send()

    @pl.loop(1, devices)
    def _(d):
        s = lax.rem(me - d + devices, devices)
        device = (s // n_col, s % n_col)
        remote(qa.at[0], ra.at[s], a_send.at[0], a_recv.at[s], device).wait_recv()
        remote(meta.at[0], rm.at[s], m_send.at[0], m_recv.at[s], device).wait_recv()

    got = jnp.max(rm[...], axis=1)
    take = lax.broadcasted_iota(jnp.int32, (128, packed), 0)
    at = lax.broadcasted_iota(jnp.int32, (128, packed), 1) % pad
    mine = (lax.broadcasted_iota(jnp.int32, (devices, packed), 0)
            == lax.broadcasted_iota(jnp.int32, (devices, packed), 1) // pad)

    def lanes(offset):
        full = jnp.dot(got, (take == at + offset).astype(jnp.float32), precision=HIGHEST,
                       preferred_element_type=jnp.float32)
        return jnp.sum(jnp.where(mine, full, 0.0), axis=0, keepdims=True)

    scale_lane = lanes(0)
    slot_lane = jnp.round(lanes(64)).astype(jnp.int32)
    put = jnp.where(lax.broadcasted_iota(jnp.int32, (own, packed), 0) == slot_lane, scale_lane, 0.0).astype(jnp.bfloat16)
    high, low = split(ra[...].reshape(packed, rank))
    placed = (jnp.dot(put, high, preferred_element_type=jnp.float32)
              + jnp.dot(put, low, preferred_element_type=jnp.float32))
    out_ref[...] = jnp.dot(placed, ginv_ref[...], precision=HIGHEST, preferred_element_type=jnp.float32)

    @pl.loop(1, devices)
    def _(d):
        for copy in out_copies(d):
            copy.wait_send()


def per_device(n_row, n_col, tiles, tile_coord, tile_count, factors, owner, gram_inverse):
    own, rank = factors.shape
    tile_dim = tiles.shape[-1]
    slots = tiles.shape[2]
    devices = n_row * n_col
    row_tiles = own * n_col // tile_dim
    col_tiles = own * n_row // tile_dim
    tpd = own // tile_dim
    r = lax.axis_index("row")
    c = lax.axis_index("col")
    dma = pltpu.SemaphoreType.DMA

    panel = pl.pallas_call(
        functools.partial(gather_kernel, n_row, n_col),
        out_shape=jax.ShapeDtypeStruct((n_col + n_row, own, rank), factors.dtype),
        in_specs=[ANY],
        out_specs=ANY,
        scratch_shapes=[
            dma((n_col // 2,)), dma((n_col // 2,)), dma, dma((n_row,)),
            dma((n_col,)), dma((n_row,)), dma,
        ],
        compiler_params=pltpu.CompilerParams(collective_id=0, has_side_effects=True),
        name="gather",
    )(factors)

    per_step = 8
    steps = slots // per_step
    count = tile_count[0, 0]
    ratio = n_col // n_row
    first = jnp.where(r == c // ratio, (c % ratio) * col_tiles, row_tiles)
    numbers = jnp.stack([count, r * row_tiles, c * col_tiles, first]).astype(jnp.int32)
    whole = lambda *shape: pl.BlockSpec(shape, lambda g, a, b: (0,) * len(shape))
    qrow, qcol, srow, scol = pl.pallas_call(
        functools.partial(tile_kernel, per_step),
        out_shape=(
            jax.ShapeDtypeStruct((row_tiles, tile_dim, rank), jnp.int16),
            jax.ShapeDtypeStruct((col_tiles, tile_dim, rank), jnp.int16),
            jax.ShapeDtypeStruct((row_tiles, 1, tile_dim), jnp.float32),
            jax.ShapeDtypeStruct((col_tiles, 1, tile_dim), jnp.float32),
        ),
        grid_spec=pltpu.PrefetchScalarGridSpec(
            num_scalar_prefetch=2,
            grid=(steps,),
            in_specs=[
                pl.BlockSpec(
                    (per_step, tile_dim, tile_dim),
                    lambda g, a, b: (jnp.minimum(g, jnp.maximum(b[0] - 1, 0) // per_step), 0, 0),
                ),
                whole(row_tiles + col_tiles, tile_dim, rank),
            ],
            out_specs=(
                whole(row_tiles, tile_dim, rank),
                whole(col_tiles, tile_dim, rank),
                whole(row_tiles, 1, tile_dim),
                whole(col_tiles, 1, tile_dim),
            ),
            scratch_shapes=[
                pltpu.VMEM((row_tiles + 1, tile_dim, rank), jnp.float32),
                pltpu.VMEM((col_tiles + 1, tile_dim, rank), jnp.float32),
            ],
        ),
        compiler_params=pltpu.CompilerParams(vmem_limit_bytes=56 * MIB),
        name="tile_pass",
    )(
        tile_coord.reshape(-1), numbers, tiles.reshape(slots, tile_dim, tile_dim),
        panel.reshape(row_tiles + col_tiles, tile_dim, rank),
    )

    share = own // devices
    pad = -(-share // 16) * 16
    packed = devices * pad
    return pl.pallas_call(
        functools.partial(solve_kernel, n_row, n_col, pad, tile_dim),
        out_shape=jax.ShapeDtypeStruct((own, rank), jnp.float32),
        in_specs=[ANY, ANY, ANY, ANY, VMEM, VMEM, VMEM],
        out_specs=VMEM,
        scratch_shapes=[
            pltpu.VMEM((n_col, own, rank), jnp.int16),
            pltpu.VMEM((n_col * tpd, 1, tile_dim), jnp.float32),
            pltpu.VMEM((n_row, own, rank), jnp.int16),
            pltpu.VMEM((n_row * tpd, 1, tile_dim), jnp.float32),
            pltpu.VMEM((n_row, own, rank), jnp.int16),
            pltpu.VMEM((n_row * tpd, 1, tile_dim), jnp.float32),
            pltpu.VMEM((packed, own), jnp.float32),
            pltpu.VMEM((packed, rank), jnp.float32),
            pltpu.VMEM((devices, pad, rank), jnp.int16),
            pltpu.VMEM((devices, 8, 128), jnp.float32),
            pltpu.VMEM((devices, pad, rank), jnp.int16),
            pltpu.VMEM((devices, 8, 128), jnp.float32),
            dma((n_col,)), dma((n_col,)), dma((n_row,)), dma((n_row,)),
            dma((n_col,)), dma((n_col,)), dma((n_row,)), dma((n_row,)),
            dma((n_row,)), dma((n_row,)), dma((n_row,)), dma((n_row,)),
            dma((devices,)), dma((devices,)), dma((devices,)), dma((devices,)), dma((2,)),
        ],
        compiler_params=pltpu.CompilerParams(
            collective_id=1, has_side_effects=True, vmem_limit_bytes=40 * MIB),
        name="solve",
    )(
        qrow.reshape(n_col, own, rank), qcol.reshape(n_row, own, rank), srow, scol,
        owner.reshape(1, own), owner.reshape(own, 1), gram_inverse,
    )


def solution(mesh):
    in_specs = (
        P("row", "col", None, None, None),
        P("row", "col", None, None),
        P("row", "col"),
        P(("row", "col"), None),
        P(("row", "col")),
        P(),
    )
    out_specs = P(("row", "col"), None)
    return jax.shard_map(
        functools.partial(per_device, mesh.shape["row"], mesh.shape["col"]),
        mesh=mesh, in_specs=in_specs, out_specs=out_specs, check_vma=False,
    )
```

```python
import functools

import jax
import jax.numpy as jnp
from jax import lax
from jax.experimental import pallas as pl
from jax.experimental.pallas import tpu as pltpu
from jax.sharding import PartitionSpec as P

MESH = pl.DeviceIdType.MESH
ANY = pl.BlockSpec(memory_space=pl.ANY)
VMEM = pl.BlockSpec(memory_space=pltpu.VMEM)
HIGHEST = lax.Precision.HIGHEST
MIB = 1 << 20
PARTS = 4


def remote(src, dst, send_sem, recv_sem, device):
    return pltpu.make_async_remote_copy(
        src_ref=src, dst_ref=dst, send_sem=send_sem, recv_sem=recv_sem,
        device_id=device, device_id_type=MESH,
    )


def gather_kernel(n_row, n_col, f_ref, row_ref, row_send, fwd_send, pair_send, col_send,
                  row_recv, col_recv, local_sem):
    r = lax.axis_index("row")
    c = lax.axis_index("col")
    ratio = n_col // n_row
    chips = n_col // 2
    k, e = c // 2, c % 2
    partner = c + 1 - 2 * e
    used = k >= r * ratio // 2
    up = c // ratio

    barrier = pltpu.get_barrier_semaphore()
    for j in range(1, n_col):
        pl.semaphore_signal(barrier, inc=1, device_id=(r, lax.rem(c + j, n_col)), device_id_type=MESH)
    for d in range(1, n_row):
        @pl.when(r - d >= 0)
        def _(d=d):
            pl.semaphore_signal(barrier, inc=1, device_id=(r - d, r * ratio + c // n_row), device_id_type=MESH)

    @pl.when(r < up)
    def _():
        for i in range(n_row):
            pl.semaphore_signal(barrier, inc=1, device_id=(up, (c % ratio) * n_row + i), device_id_type=MESH)
    pl.semaphore_wait(barrier, n_col - 1 + r + jnp.where(r < up, n_row, 0))

    def row_copy(j):
        return remote(f_ref, row_ref.at[c], row_send.at[j], row_recv.at[c],
                      (r, 2 * lax.rem(k + j, chips) + e))

    def row_goes(j):
        return lax.rem(k + j, chips) >= r * ratio // 2

    def col_copy(d):
        return remote(f_ref, row_ref.at[n_col + c % n_row], col_send.at[d], col_recv.at[c % n_row],
                      (r - d, r * ratio + c // n_row))

    for j in range(1, chips):
        @pl.when(row_goes(j))
        def _(j=j):
            row_copy(j).start()
    for d in range(n_row - 1, 0, -1):
        @pl.when(r - d >= 0)
        def _(d=d):
            col_copy(d).start()

    def source(j):
        return 2 * lax.rem(k - j + chips, chips)

    def forward(j):
        s = source(j) + e
        return remote(row_ref.at[s], row_ref.at[s], fwd_send.at[j], row_recv.at[s], (r, partner))

    def arrival(s):
        return remote(f_ref, row_ref.at[s], row_send.at[0], row_recv.at[s], (r, partner))

    @pl.when(used)
    def _():
        own = pltpu.make_async_copy(f_ref, row_ref.at[c], local_sem)
        own.start()
        pair = remote(f_ref, row_ref.at[c], pair_send, row_recv.at[c], (r, partner))
        pair.start()
        for j in range(1, chips):
            arrival(source(j) + e).wait_recv()
            forward(j).start()
        arrival(partner).wait_recv()
        for j in range(1, chips):
            arrival(source(j) + 1 - e).wait_recv()
        own.wait()
        pair.wait_send()
        for j in range(1, chips):
            forward(j).wait_send()

    for j in range(1, chips):
        @pl.when(row_goes(j))
        def _(j=j):
            row_copy(j).wait_send()
    for d in range(n_row - 1, 0, -1):
        @pl.when(r - d >= 0)
        def _(d=d):
            col_copy(d).wait_send()

    @pl.when(r < up)
    def _():
        for i in range(n_row):
            remote(f_ref, row_ref.at[n_col + i], col_send.at[0], col_recv.at[i], (r, partner)).wait_recv()


def encode(x):
    most = jnp.max(jnp.abs(x), axis=1, keepdims=True)
    scale = jnp.maximum(most * (1.01 / 32767.0), 1e-30).astype(jnp.bfloat16).astype(jnp.float32)
    coded = jnp.round(x * (1.0 / scale)).astype(jnp.int32).astype(jnp.int16)
    return coded, scale


def split(coded):
    v = coded.astype(jnp.int32)
    high = (v + 128) >> 8
    low = v - (high << 8)
    return (
        (high << 8).astype(jnp.float32).astype(jnp.bfloat16),
        low.astype(jnp.float32).astype(jnp.bfloat16),
    )


def tile_kernel(per_step, coord_ref, meta_ref, tiles_ref, panel_ref,
                qrow_ref, qcol_ref, srow_ref, scol_ref, row_sum, col_sum):
    step = pl.program_id(0)
    count = meta_ref[0]
    tile_dim = tiles_ref.shape[-1]
    row_tiles = qrow_ref.shape[0]
    col_tiles = qcol_ref.shape[0]

    @pl.when(step == 0)
    def _():
        row_sum[...] = jnp.zeros_like(row_sum)
        col_sum[...] = jnp.zeros_like(col_sum)

    @pl.when(step * per_step < count)
    def _():
        for s in range(per_step):
            slot = step * per_step + s
            live = slot < count
            i = jnp.where(live, coord_ref[2 * slot], 0)
            j = jnp.where(live, coord_ref[2 * slot + 1], 0)
            upper = live & (meta_ref[1] + i < meta_ref[2] + j)
            tile = tiles_ref[s]
            row_term = jnp.dot(tile, panel_ref[meta_ref[3] + j], preferred_element_type=jnp.float32)
            col_term = lax.dot_general(
                tile, panel_ref[i], (((0,), (0,)), ((), ())), preferred_element_type=jnp.float32)
            row_sum[jnp.where(live, i, row_tiles)] += row_term
            col_sum[jnp.where(upper, j, col_tiles)] += col_term

    @pl.when(step == pl.num_programs(0) - 1)
    def _():
        eye = (lax.broadcasted_iota(jnp.int32, (tile_dim, tile_dim), 0)
               == lax.broadcasted_iota(jnp.int32, (tile_dim, tile_dim), 1))

        def code(total, coded_ref, scale_ref):
            @pl.loop(0, coded_ref.shape[0], unroll=4)
            def _(t):
                coded, scale = encode(total[t])
                coded_ref[t] = coded
                scale_ref[t] = jnp.sum(jnp.where(eye, scale, 0.0), axis=0, keepdims=True)

        code(row_sum, qrow_ref, srow_ref)
        code(col_sum, qcol_ref, scol_ref)


def solve_kernel(n_row, n_col, pad, tile_dim, qrow_ref, qcol_ref, srow_ref, scol_ref, owner_lane, owner_sub, ginv_ref,
                 out_ref, rq, rs, oq, pq, ps, eq, es, cq, cs, hq, hs, pick, total, qa, meta, ra, rm,
                 pq_send, ps_send, pq_recv, ps_recv, oq_sem, row_send, rsc_send, col_send, csc_send, row_recv, rsc_recv, col_recv, csc_recv,
                 hq_send, hs_send, hq_recv, hs_recv, a_send, m_send, a_recv, m_recv, local_sem):
    r = lax.axis_index("row")
    c = lax.axis_index("col")
    me = r * n_col + c
    devices = n_row * n_col
    ratio = n_col // n_row
    own, rank = out_ref.shape
    tpd = own // tile_dim
    packed = devices * pad
    up = c // ratio
    used = r <= up

    barrier = pltpu.get_barrier_semaphore()

    @pl.loop(1, devices)
    def _(d):
        to = lax.rem(me + d, devices)
        pl.semaphore_signal(barrier, inc=1, device_id=(to // n_col, to % n_col), device_id_type=MESH)
    pl.semaphore_wait(barrier, devices - 1)

    chips = n_col // 2
    k, e = c // 2, c % 2
    partner = c + 1 - 2 * e

    def tiles_of(m):
        return pl.ds(m * tpd, tpd)

    def pair_copies(m):
        to = 2 * m + 1 - e
        return (
            remote(qrow_ref.at[to], pq.at[m], pq_send.at[m], pq_recv.at[m], (r, partner)),
            remote(srow_ref.at[tiles_of(to)], ps.at[tiles_of(m)], ps_send.at[m], ps_recv.at[m], (r, partner)),
        )

    def own_copy(m):
        return pltpu.make_async_copy(qrow_ref.at[2 * m + e], oq.at[m], oq_sem.at[m])

    def row_copies(m):
        to = (r, 2 * m + e)
        return (
            remote(eq.at[m], rq.at[k], row_send.at[m], row_recv.at[k], to),
            remote(es.at[tiles_of(m)], rs.at[tiles_of(k)], rsc_send.at[m], rsc_recv.at[k], to),
        )

    def rows_of(p):
        return pl.ds(p * (own // PARTS), own // PARTS)

    def relay_copies(i, p):
        to = (r, (c % ratio) * n_row + i)
        values = remote(qcol_ref.at[i, rows_of(p)], hq.at[up, rows_of(p)],
                        col_send.at[i, p], hq_recv.at[up, p], to)
        scales = remote(scol_ref.at[pl.ds(i * tpd, tpd)], hs.at[pl.ds(up * tpd, tpd)],
                        csc_send.at[i], hs_recv.at[up], to)
        return (scales, values) if p == 0 else (values,)

    def hop_copies(u, p):
        values = remote(hq.at[u, rows_of(p)], cq.at[r, rows_of(p)], hq_send.at[u, p], col_recv.at[r, p], (u, c))
        scales = remote(hs.at[pl.ds(u * tpd, tpd)], cs.at[pl.ds(r * tpd, tpd)],
                        hs_send.at[u], csc_recv.at[r], (u, c))
        return (scales, values) if p == 0 else (values,)

    def relay_arrival(u, p):
        device = (r, ratio * u + c // n_row)
        remote(qcol_ref.at[0, rows_of(p)], hq.at[u, rows_of(p)], col_send.at[0, p], hq_recv.at[u, p],
               device).wait_recv()
        if p == 0:
            remote(scol_ref.at[pl.ds(0, tpd)], hs.at[pl.ds(u * tpd, tpd)], csc_send.at[0], hs_recv.at[u],
                   device).wait_recv()

    def hops(u):
        return (u > r) & (ratio * u + c // n_row != c)

    def col_copies(i, p):
        to = (up, (c % ratio) * n_row + i)
        values = remote(qcol_ref.at[i, rows_of(p)], cq.at[r, rows_of(p)], col_send.at[i, p], col_recv.at[r, p], to)
        scales = remote(scol_ref.at[pl.ds(i * tpd, tpd)], cs.at[pl.ds(r * tpd, tpd)],
                        csc_send.at[i], csc_recv.at[r], to)
        return (scales, values) if p == 0 else (values,)

    def col_here(i):
        return tuple(
            pltpu.make_async_copy(qcol_ref.at[i, rows_of(p)], cq.at[r, rows_of(p)], col_recv.at[r, p])
            for p in range(PARTS)
        ) + (
            pltpu.make_async_copy(scol_ref.at[pl.ds(i * tpd, tpd)], cs.at[pl.ds(r * tpd, tpd)], csc_recv.at[r]),
        )

    def stays(i):
        return (c % ratio) * n_row + i == c

    def col_mine(i):
        return (r == up) & stays(i)

    def col_relayed(i):
        return (r < up) & jnp.logical_not(stays(i))

    def col_direct(i):
        return (r <= up) & jnp.logical_not(col_mine(i)) & jnp.logical_not(col_relayed(i))

    @pl.when(used)
    def _():
        for p in range(PARTS):
            for i in range(n_row):
                @pl.when(col_relayed(i))
                def _(i=i, p=p):
                    for copy in relay_copies(i, p):
                        copy.start()

                @pl.when(col_direct(i))
                def _(i=i, p=p):
                    for copy in col_copies(i, p):
                        copy.start()
        for i in range(n_row):
            @pl.when(col_mine(i))
            def _(i=i):
                for copy in col_here(i):
                    copy.start()
        for j in range(1, chips + 1):
            m = lax.rem(k + j, chips)
            own_copy(m).start()
            for copy in pair_copies(m):
                copy.start()

    ow = owner_lane[...]
    dest = ow // own
    slot = (ow - dest * own).astype(jnp.float32)
    same = (owner_sub[...] // own == dest) & (
        lax.broadcasted_iota(jnp.int32, (own, own), 0) < lax.broadcasted_iota(jnp.int32, (own, own), 1))
    place = dest * pad + jnp.sum(same.astype(jnp.int32), axis=0, keepdims=True)
    chosen = lax.broadcasted_iota(jnp.int32, (packed, own), 0) == place
    pick[...] = chosen.astype(jnp.float32)
    slot_sub = jnp.sum(jnp.where(chosen, slot, 0.0), axis=1, keepdims=True)
    total[...] = jnp.zeros_like(total)

    eye = (lax.broadcasted_iota(jnp.int32, (tile_dim, tile_dim), 0)
           == lax.broadcasted_iota(jnp.int32, (tile_dim, tile_dim), 1))

    def decode(coded, scale):
        down = jnp.sum(jnp.where(eye, scale, 0.0), axis=1, keepdims=True)
        return coded.astype(jnp.int32).astype(jnp.float32) * down

    def pair_sum(j):
        @pl.when(used)
        def _():
            m = lax.rem(k + j, chips)
            own_copy(m).wait()
            for copy in pair_copies(m):
                copy.wait_recv()
            for t in range(tpd):
                words = pl.ds(t * tile_dim, tile_dim)
                both = (decode(oq[m, words, :], srow_ref[(2 * m + e) * tpd + t])
                        + decode(pq[m, words, :], ps[m * tpd + t]))
                coded, scale = encode(both)
                eq[m, words, :] = coded
                es[m * tpd + t] = jnp.sum(jnp.where(eye, scale, 0.0), axis=0, keepdims=True)
            for copy in row_copies(m):
                copy.start()

    def relay(p):
        for u in range(n_row - 1, 0, -1):
            @pl.when(hops(u))
            def _(u=u):
                relay_arrival(u, p)
                for copy in hop_copies(u, p):
                    copy.start()

    for n in range(max(chips - 1, PARTS)):
        if n < chips - 1:
            pair_sum(n + 1)
        if n < PARTS:
            relay(n)

    def add(coded_ref, scales_ref, s, at=None):
        for t in range(tpd):
            words = pl.ds(t * tile_dim, tile_dim)
            scaled = (pick[:, words] * scales_ref[(s if at is None else at) * tpd + t]).astype(jnp.bfloat16)
            high, low = split(coded_ref[s, words, :])
            total[...] += (jnp.dot(scaled, high, preferred_element_type=jnp.float32)
                           + jnp.dot(scaled, low, preferred_element_type=jnp.float32))

    def row_arrival(s):
        remote(eq.at[0], rq.at[s], row_send.at[0], row_recv.at[s], (r, 2 * s + e)).wait_recv()
        remote(es.at[tiles_of(0)], rs.at[tiles_of(s)], rsc_send.at[0], rsc_recv.at[s], (r, 2 * s + e)).wait_recv()

    def col_arrival(s):
        for p in range(PARTS):
            remote(qcol_ref.at[0, rows_of(p)], cq.at[s, rows_of(p)], col_send.at[0, p], col_recv.at[s, p],
                   (s, c)).wait_recv()
        remote(scol_ref.at[pl.ds(0, tpd)], cs.at[pl.ds(s * tpd, tpd)], csc_send.at[0], csc_recv.at[s],
               (s, c)).wait_recv()

    @pl.when(used)
    def _():
        own_copy(k).wait()
        for copy in pair_copies(k):
            copy.wait_recv()
        add(oq, srow_ref, k, c)
        add(pq, ps, k)

    for j in range(1, chips):
        s = lax.rem(k - j + chips, chips)

        @pl.when(s >= r * ratio // 2)
        def _(s=s):
            row_arrival(s)
            add(rq, rs, s)

    for d in range(n_row):
        @pl.when(r - d >= 0)
        def _(d=d):
            if d == 0:
                mine = c == (r * ratio + c // n_row)

                @pl.when(mine)
                def _():
                    for copy in col_here(c % n_row):
                        copy.wait()

                @pl.when(jnp.logical_not(mine))
                def _():
                    col_arrival(r)
            else:
                col_arrival(r - d)
            add(cq, cs, r - d)

    coded, scale = encode(total[...])
    qa[...] = coded.reshape(devices, pad, rank)
    lane = lax.broadcasted_iota(jnp.int32, (packed, 128), 1)
    within = lax.broadcasted_iota(jnp.int32, (packed, 128), 0) % pad
    spread = jnp.where(lane == within, scale, 0.0) + jnp.where(lane == within + 64, slot_sub, 0.0)
    meta[...] = jnp.broadcast_to(
        jnp.sum(spread.reshape(devices, pad, 128), axis=1, keepdims=True), meta.shape)

    def out_copies(d):
        to = lax.rem(me + d, devices)
        device = (to // n_col, to % n_col)
        return (
            remote(qa.at[to], ra.at[me], a_send.at[d], a_recv.at[me], device),
            remote(meta.at[to], rm.at[me], m_send.at[d], m_recv.at[me], device),
        )

    @pl.loop(1, devices)
    def _(d):
        for copy in out_copies(d):
            copy.start()
    here = (
        pltpu.make_async_copy(qa.at[me], ra.at[me], local_sem.at[0]),
        pltpu.make_async_copy(meta.at[me], rm.at[me], local_sem.at[1]),
    )
    for copy in here:
        copy.start()
    for copy in here:
        copy.wait()

    @pl.when(used)
    def _():
        for i in range(n_row):
            @pl.when(col_relayed(i))
            def _(i=i):
                for p in range(PARTS):
                    for copy in relay_copies(i, p):
                        copy.wait_send()

            @pl.when(col_direct(i))
            def _(i=i):
                for p in range(PARTS):
                    for copy in col_copies(i, p):
                        copy.wait_send()
        for j in range(1, chips):
            for copy in row_copies(lax.rem(k + j, chips)):
                copy.wait_send()
        for m in range(chips):
            for copy in pair_copies(m):
                copy.wait_send()

    for u in range(n_row - 1, 0, -1):
        @pl.when(hops(u))
        def _(u=u):
            for p in range(PARTS):
                for copy in hop_copies(u, p):
                    copy.wait_send()

    @pl.loop(1, devices)
    def _(d):
        s = lax.rem(me - d + devices, devices)
        device = (s // n_col, s % n_col)
        remote(qa.at[0], ra.at[s], a_send.at[0], a_recv.at[s], device).wait_recv()
        remote(meta.at[0], rm.at[s], m_send.at[0], m_recv.at[s], device).wait_recv()

    got = jnp.max(rm[...], axis=1)
    take = lax.broadcasted_iota(jnp.int32, (128, packed), 0)
    at = lax.broadcasted_iota(jnp.int32, (128, packed), 1) % pad
    mine = (lax.broadcasted_iota(jnp.int32, (devices, packed), 0)
            == lax.broadcasted_iota(jnp.int32, (devices, packed), 1) // pad)

    def lanes(offset):
        full = jnp.dot(got, (take == at + offset).astype(jnp.float32), precision=HIGHEST,
                       preferred_element_type=jnp.float32)
        return jnp.sum(jnp.where(mine, full, 0.0), axis=0, keepdims=True)

    scale_lane = lanes(0)
    slot_lane = jnp.round(lanes(64)).astype(jnp.int32)
    put = jnp.where(lax.broadcasted_iota(jnp.int32, (own, packed), 0) == slot_lane, scale_lane, 0.0).astype(jnp.bfloat16)
    high, low = split(ra[...].reshape(packed, rank))
    placed = (jnp.dot(put, high, preferred_element_type=jnp.float32)
              + jnp.dot(put, low, preferred_element_type=jnp.float32))
    out_ref[...] = jnp.dot(placed, ginv_ref[...], precision=HIGHEST, preferred_element_type=jnp.float32)

    @pl.loop(1, devices)
    def _(d):
        for copy in out_copies(d):
            copy.wait_send()


def per_device(n_row, n_col, tiles, tile_coord, tile_count, factors, owner, gram_inverse):
    own, rank = factors.shape
    tile_dim = tiles.shape[-1]
    slots = tiles.shape[2]
    devices = n_row * n_col
    row_tiles = own * n_col // tile_dim
    col_tiles = own * n_row // tile_dim
    tpd = own // tile_dim
    r = lax.axis_index("row")
    c = lax.axis_index("col")
    dma = pltpu.SemaphoreType.DMA

    panel = pl.pallas_call(
        functools.partial(gather_kernel, n_row, n_col),
        out_shape=jax.ShapeDtypeStruct((n_col + n_row, own, rank), factors.dtype),
        in_specs=[ANY],
        out_specs=ANY,
        scratch_shapes=[
            dma((n_col // 2,)), dma((n_col // 2,)), dma, dma((n_row,)),
            dma((n_col,)), dma((n_row,)), dma,
        ],
        compiler_params=pltpu.CompilerParams(collective_id=0, has_side_effects=True),
        name="gather",
    )(factors)

    per_step = 8
    steps = slots // per_step
    count = tile_count[0, 0]
    ratio = n_col // n_row
    first = jnp.where(r == c // ratio, (c % ratio) * col_tiles, row_tiles)
    numbers = jnp.stack([count, r * row_tiles, c * col_tiles, first]).astype(jnp.int32)
    whole = lambda *shape: pl.BlockSpec(shape, lambda g, a, b: (0,) * len(shape))
    qrow, qcol, srow, scol = pl.pallas_call(
        functools.partial(tile_kernel, per_step),
        out_shape=(
            jax.ShapeDtypeStruct((row_tiles, tile_dim, rank), jnp.int16),
            jax.ShapeDtypeStruct((col_tiles, tile_dim, rank), jnp.int16),
            jax.ShapeDtypeStruct((row_tiles, 1, tile_dim), jnp.float32),
            jax.ShapeDtypeStruct((col_tiles, 1, tile_dim), jnp.float32),
        ),
        grid_spec=pltpu.PrefetchScalarGridSpec(
            num_scalar_prefetch=2,
            grid=(steps,),
            in_specs=[
                pl.BlockSpec(
                    (per_step, tile_dim, tile_dim),
                    lambda g, a, b: (jnp.minimum(g, jnp.maximum(b[0] - 1, 0) // per_step), 0, 0),
                ),
                whole(row_tiles + col_tiles, tile_dim, rank),
            ],
            out_specs=(
                whole(row_tiles, tile_dim, rank),
                whole(col_tiles, tile_dim, rank),
                whole(row_tiles, 1, tile_dim),
                whole(col_tiles, 1, tile_dim),
            ),
            scratch_shapes=[
                pltpu.VMEM((row_tiles + 1, tile_dim, rank), jnp.float32),
                pltpu.VMEM((col_tiles + 1, tile_dim, rank), jnp.float32),
            ],
        ),
        compiler_params=pltpu.CompilerParams(vmem_limit_bytes=56 * MIB),
        name="tile_pass",
    )(
        tile_coord.reshape(-1), numbers, tiles.reshape(slots, tile_dim, tile_dim),
        panel.reshape(row_tiles + col_tiles, tile_dim, rank),
    )

    share = own // devices
    chips = n_col // 2
    pad = -(-share // 16) * 16
    packed = devices * pad
    return pl.pallas_call(
        functools.partial(solve_kernel, n_row, n_col, pad, tile_dim),
        out_shape=jax.ShapeDtypeStruct((own, rank), jnp.float32),
        in_specs=[ANY, ANY, VMEM, ANY, VMEM, VMEM, VMEM],
        out_specs=VMEM,
        scratch_shapes=[
            pltpu.VMEM((chips, own, rank), jnp.int16),
            pltpu.VMEM((chips * tpd, 1, tile_dim), jnp.float32),
            pltpu.VMEM((chips, own, rank), jnp.int16),
            pltpu.VMEM((chips, own, rank), jnp.int16),
            pltpu.VMEM((chips * tpd, 1, tile_dim), jnp.float32),
            pltpu.VMEM((chips, own, rank), jnp.int16),
            pltpu.VMEM((chips * tpd, 1, tile_dim), jnp.float32),
            pltpu.VMEM((n_row, own, rank), jnp.int16),
            pltpu.VMEM((n_row * tpd, 1, tile_dim), jnp.float32),
            pltpu.VMEM((n_row, own, rank), jnp.int16),
            pltpu.VMEM((n_row * tpd, 1, tile_dim), jnp.float32),
            pltpu.VMEM((packed, own), jnp.float32),
            pltpu.VMEM((packed, rank), jnp.float32),
            pltpu.VMEM((devices, pad, rank), jnp.int16),
            pltpu.VMEM((devices, 8, 128), jnp.float32),
            pltpu.VMEM((devices, pad, rank), jnp.int16),
            pltpu.VMEM((devices, 8, 128), jnp.float32),
            dma((chips,)), dma((chips,)), dma((chips,)), dma((chips,)), dma((chips,)),
            dma((chips,)), dma((chips,)), dma((n_row, PARTS)), dma((n_row,)),
            dma((chips,)), dma((chips,)), dma((n_row, PARTS)), dma((n_row,)),
            dma((n_row, PARTS)), dma((n_row,)), dma((n_row, PARTS)), dma((n_row,)),
            dma((devices,)), dma((devices,)), dma((devices,)), dma((devices,)), dma((2,)),
        ],
        compiler_params=pltpu.CompilerParams(
            collective_id=1, has_side_effects=True, vmem_limit_bytes=60 * MIB),
        name="solve",
    )(
        qrow.reshape(n_col, own, rank), qcol.reshape(n_row, own, rank), srow, scol,
        owner.reshape(1, own), owner.reshape(own, 1), gram_inverse,
    )


def solution(mesh):
    in_specs = (
        P("row", "col", None, None, None),
        P("row", "col", None, None),
        P("row", "col"),
        P(("row", "col"), None),
        P(("row", "col")),
        P(),
    )
    out_specs = P(("row", "col"), None)
    return jax.shard_map(
        functools.partial(per_device, mesh.shape["row"], mesh.shape["col"]),
        mesh=mesh, in_specs=in_specs, out_specs=out_specs, check_vma=False,
    )
```

```python
import functools

import jax
import jax.numpy as jnp
from jax import lax
from jax.experimental import pallas as pl
from jax.experimental.pallas import tpu as pltpu
from jax.sharding import PartitionSpec as P

MESH = pl.DeviceIdType.MESH
ANY = pl.BlockSpec(memory_space=pl.ANY)
VMEM = pl.BlockSpec(memory_space=pltpu.VMEM)
HIGHEST = lax.Precision.HIGHEST
MIB = 1 << 20
PARTS = 4


def remote(src, dst, send_sem, recv_sem, device):
    return pltpu.make_async_remote_copy(
        src_ref=src, dst_ref=dst, send_sem=send_sem, recv_sem=recv_sem,
        device_id=device, device_id_type=MESH,
    )


def gather_kernel(n_row, n_col, f_ref, row_ref, row_send, fwd_send, pair_send, col_send,
                  row_recv, col_recv, local_sem):
    r = lax.axis_index("row")
    c = lax.axis_index("col")
    ratio = n_col // n_row
    chips = n_col // 2
    k, e = c // 2, c % 2
    partner = c + 1 - 2 * e
    used = k >= r * ratio // 2
    up = c // ratio

    barrier = pltpu.get_barrier_semaphore()
    for j in range(1, n_col):
        pl.semaphore_signal(barrier, inc=1, device_id=(r, lax.rem(c + j, n_col)), device_id_type=MESH)
    for d in range(1, n_row):
        @pl.when(r - d >= 0)
        def _(d=d):
            pl.semaphore_signal(barrier, inc=1, device_id=(r - d, r * ratio + c // n_row), device_id_type=MESH)

    @pl.when(r < up)
    def _():
        for i in range(n_row):
            pl.semaphore_signal(barrier, inc=1, device_id=(up, (c % ratio) * n_row + i), device_id_type=MESH)
    pl.semaphore_wait(barrier, n_col - 1 + r + jnp.where(r < up, n_row, 0))

    def row_copy(j):
        return remote(f_ref, row_ref.at[c], row_send.at[j], row_recv.at[c],
                      (r, 2 * lax.rem(k + j, chips) + e))

    def row_goes(j):
        return lax.rem(k + j, chips) >= r * ratio // 2

    def col_copy(d):
        return remote(f_ref, row_ref.at[n_col + c % n_row], col_send.at[d], col_recv.at[c % n_row],
                      (r - d, r * ratio + c // n_row))

    for j in range(1, chips):
        @pl.when(row_goes(j))
        def _(j=j):
            row_copy(j).start()
    for d in range(n_row - 1, 0, -1):
        @pl.when(r - d >= 0)
        def _(d=d):
            col_copy(d).start()

    def source(j):
        return 2 * lax.rem(k - j + chips, chips)

    def forward(j):
        s = source(j) + e
        return remote(row_ref.at[s], row_ref.at[s], fwd_send.at[j], row_recv.at[s], (r, partner))

    def arrival(s):
        return remote(f_ref, row_ref.at[s], row_send.at[0], row_recv.at[s], (r, partner))

    @pl.when(used)
    def _():
        own = pltpu.make_async_copy(f_ref, row_ref.at[c], local_sem)
        own.start()
        pair = remote(f_ref, row_ref.at[c], pair_send, row_recv.at[c], (r, partner))
        pair.start()
        for j in range(1, chips):
            arrival(source(j) + e).wait_recv()
            forward(j).start()
        arrival(partner).wait_recv()
        for j in range(1, chips):
            arrival(source(j) + 1 - e).wait_recv()
        own.wait()
        pair.wait_send()
        for j in range(1, chips):
            forward(j).wait_send()

    for j in range(1, chips):
        @pl.when(row_goes(j))
        def _(j=j):
            row_copy(j).wait_send()
    for d in range(n_row - 1, 0, -1):
        @pl.when(r - d >= 0)
        def _(d=d):
            col_copy(d).wait_send()

    @pl.when(r < up)
    def _():
        for i in range(n_row):
            remote(f_ref, row_ref.at[n_col + i], col_send.at[0], col_recv.at[i], (r, partner)).wait_recv()


def encode(x):
    most = jnp.max(jnp.abs(x), axis=1, keepdims=True)
    scale = jnp.maximum(most * (1.01 / 32767.0), 1e-30).astype(jnp.bfloat16).astype(jnp.float32)
    coded = jnp.round(x * (1.0 / scale)).astype(jnp.int32).astype(jnp.int16)
    return coded, scale


def split(coded):
    v = coded.astype(jnp.int32)
    high = (v + 128) >> 8
    low = v - (high << 8)
    return (
        (high << 8).astype(jnp.float32).astype(jnp.bfloat16),
        low.astype(jnp.float32).astype(jnp.bfloat16),
    )


def tile_kernel(per_step, coord_ref, meta_ref, tiles_ref, panel_ref,
                qrow_ref, qcol_ref, srow_ref, scol_ref, row_sum, col_sum):
    step = pl.program_id(0)
    count = meta_ref[0]
    tile_dim = tiles_ref.shape[-1]
    row_tiles = qrow_ref.shape[0]
    col_tiles = qcol_ref.shape[0]

    @pl.when(step == 0)
    def _():
        row_sum[...] = jnp.zeros_like(row_sum)
        col_sum[...] = jnp.zeros_like(col_sum)

    @pl.when(step * per_step < count)
    def _():
        for s in range(per_step):
            slot = step * per_step + s
            live = slot < count
            i = jnp.where(live, coord_ref[2 * slot], 0)
            j = jnp.where(live, coord_ref[2 * slot + 1], 0)
            upper = live & (meta_ref[1] + i < meta_ref[2] + j)
            tile = tiles_ref[s]
            row_term = jnp.dot(tile, panel_ref[meta_ref[3] + j], preferred_element_type=jnp.float32)
            col_term = lax.dot_general(
                tile, panel_ref[i], (((0,), (0,)), ((), ())), preferred_element_type=jnp.float32)
            row_sum[jnp.where(live, i, row_tiles)] += row_term
            col_sum[jnp.where(upper, j, col_tiles)] += col_term

    @pl.when(step == pl.num_programs(0) - 1)
    def _():
        eye = (lax.broadcasted_iota(jnp.int32, (tile_dim, tile_dim), 0)
               == lax.broadcasted_iota(jnp.int32, (tile_dim, tile_dim), 1))

        def code(total, coded_ref, scale_ref):
            @pl.loop(0, coded_ref.shape[0], unroll=4)
            def _(t):
                coded, scale = encode(total[t])
                coded_ref[t] = coded
                scale_ref[t] = jnp.sum(jnp.where(eye, scale, 0.0), axis=0, keepdims=True)

        code(row_sum, qrow_ref, srow_ref)
        code(col_sum, qcol_ref, scol_ref)


def solve_kernel(n_row, n_col, pad, tile_dim, qrow_ref, qcol_ref, srow_ref, scol_ref, owner_lane, owner_sub, ginv_ref,
                 out_ref, rq, rs, oq, pq, ps, eq, es, cq, cs, hq, hs, pick, total, qa, meta, ra, rm,
                 pq_send, ps_send, pq_recv, ps_recv, oq_sem, row_send, rsc_send, col_send, csc_send, row_recv, rsc_recv, col_recv, csc_recv,
                 hq_send, hs_send, hq_recv, hs_recv, a_send, m_send, a_recv, m_recv, local_sem):
    r = lax.axis_index("row")
    c = lax.axis_index("col")
    me = r * n_col + c
    devices = n_row * n_col
    ratio = n_col // n_row
    own, rank = out_ref.shape
    tpd = own // tile_dim
    packed = devices * pad
    up = c // ratio
    used = r <= up

    barrier = pltpu.get_barrier_semaphore()

    @pl.loop(1, devices)
    def _(d):
        to = lax.rem(me + d, devices)
        pl.semaphore_signal(barrier, inc=1, device_id=(to // n_col, to % n_col), device_id_type=MESH)
    pl.semaphore_wait(barrier, devices - 1)

    chips = n_col // 2
    k, e = c // 2, c % 2
    partner = c + 1 - 2 * e

    def tiles_of(m):
        return pl.ds(m * tpd, tpd)

    def pair_copies(m):
        to = 2 * m + 1 - e
        return (
            remote(qrow_ref.at[to], pq.at[m], pq_send.at[m], pq_recv.at[m], (r, partner)),
            remote(srow_ref.at[tiles_of(to)], ps.at[tiles_of(m)], ps_send.at[m], ps_recv.at[m], (r, partner)),
        )

    def own_copy(m):
        return pltpu.make_async_copy(qrow_ref.at[2 * m + e], oq.at[m], oq_sem.at[m])

    def row_copies(m):
        to = (r, 2 * m + e)
        return (
            remote(eq.at[m], rq.at[k], row_send.at[m], row_recv.at[k], to),
            remote(es.at[tiles_of(m)], rs.at[tiles_of(k)], rsc_send.at[m], rsc_recv.at[k], to),
        )

    def rows_of(p):
        return pl.ds(p * (own // PARTS), own // PARTS)

    def relay_copies(i, p):
        to = (r, (c % ratio) * n_row + i)
        values = remote(qcol_ref.at[i, rows_of(p)], hq.at[up, rows_of(p)],
                        col_send.at[i, p], hq_recv.at[up, p], to)
        scales = remote(scol_ref.at[pl.ds(i * tpd, tpd)], hs.at[pl.ds(up * tpd, tpd)],
                        csc_send.at[i], hs_recv.at[up], to)
        return (scales, values) if p == 0 else (values,)

    def hop_copies(u, p):
        values = remote(hq.at[u, rows_of(p)], cq.at[r, rows_of(p)], hq_send.at[u, p], col_recv.at[r, p], (u, c))
        scales = remote(hs.at[pl.ds(u * tpd, tpd)], cs.at[pl.ds(r * tpd, tpd)],
                        hs_send.at[u], csc_recv.at[r], (u, c))
        return (scales, values) if p == 0 else (values,)

    def relay_arrival(u, p):
        device = (r, ratio * u + c // n_row)
        remote(qcol_ref.at[0, rows_of(p)], hq.at[u, rows_of(p)], col_send.at[0, p], hq_recv.at[u, p],
               device).wait_recv()
        if p == 0:
            remote(scol_ref.at[pl.ds(0, tpd)], hs.at[pl.ds(u * tpd, tpd)], csc_send.at[0], hs_recv.at[u],
                   device).wait_recv()

    def hops(u):
        return (u > r) & (ratio * u + c // n_row != c)

    def col_copies(i, p):
        to = (up, (c % ratio) * n_row + i)
        values = remote(qcol_ref.at[i, rows_of(p)], cq.at[r, rows_of(p)], col_send.at[i, p], col_recv.at[r, p], to)
        scales = remote(scol_ref.at[pl.ds(i * tpd, tpd)], cs.at[pl.ds(r * tpd, tpd)],
                        csc_send.at[i], csc_recv.at[r], to)
        return (scales, values) if p == 0 else (values,)

    def col_here(i):
        return tuple(
            pltpu.make_async_copy(qcol_ref.at[i, rows_of(p)], cq.at[r, rows_of(p)], col_recv.at[r, p])
            for p in range(PARTS)
        ) + (
            pltpu.make_async_copy(scol_ref.at[pl.ds(i * tpd, tpd)], cs.at[pl.ds(r * tpd, tpd)], csc_recv.at[r]),
        )

    def stays(i):
        return (c % ratio) * n_row + i == c

    def col_mine(i):
        return (r == up) & stays(i)

    def col_relayed(i):
        return (r < up) & jnp.logical_not(stays(i))

    def col_direct(i):
        return (r <= up) & jnp.logical_not(col_mine(i)) & jnp.logical_not(col_relayed(i))

    @pl.when(used)
    def _():
        for p in range(PARTS):
            for i in range(n_row):
                @pl.when(col_relayed(i))
                def _(i=i, p=p):
                    for copy in relay_copies(i, p):
                        copy.start()

                @pl.when(col_direct(i))
                def _(i=i, p=p):
                    for copy in col_copies(i, p):
                        copy.start()
        for i in range(n_row):
            @pl.when(col_mine(i))
            def _(i=i):
                for copy in col_here(i):
                    copy.start()
        for j in range(1, chips + 1):
            m = lax.rem(k + j, chips)
            own_copy(m).start()
            for copy in pair_copies(m):
                copy.start()

    ow = owner_lane[...]
    dest = ow // own
    slot = (ow - dest * own).astype(jnp.float32)
    same = (owner_sub[...] // own == dest) & (
        lax.broadcasted_iota(jnp.int32, (own, own), 0) < lax.broadcasted_iota(jnp.int32, (own, own), 1))
    place = dest * pad + jnp.sum(same.astype(jnp.int32), axis=0, keepdims=True)
    chosen = lax.broadcasted_iota(jnp.int32, (packed, own), 0) == place
    pick[...] = chosen.astype(jnp.float32)
    slot_sub = jnp.sum(jnp.where(chosen, slot, 0.0), axis=1, keepdims=True)
    total[...] = jnp.zeros_like(total)

    eye = (lax.broadcasted_iota(jnp.int32, (tile_dim, tile_dim), 0)
           == lax.broadcasted_iota(jnp.int32, (tile_dim, tile_dim), 1))

    def decode(coded, scale):
        down = jnp.sum(jnp.where(eye, scale, 0.0), axis=1, keepdims=True)
        return coded.astype(jnp.int32).astype(jnp.float32) * down

    def pair_sum(j):
        @pl.when(used)
        def _():
            m = lax.rem(k + j, chips)
            own_copy(m).wait()
            for copy in pair_copies(m):
                copy.wait_recv()
            for t in range(tpd):
                words = pl.ds(t * tile_dim, tile_dim)
                both = (decode(oq[m, words, :], srow_ref[(2 * m + e) * tpd + t])
                        + decode(pq[m, words, :], ps[m * tpd + t]))
                coded, scale = encode(both)
                eq[m, words, :] = coded
                es[m * tpd + t] = jnp.sum(jnp.where(eye, scale, 0.0), axis=0, keepdims=True)
            for copy in row_copies(m):
                copy.start()

    def relay(p):
        for u in range(n_row - 1, 0, -1):
            @pl.when(hops(u))
            def _(u=u):
                relay_arrival(u, p)
                for copy in hop_copies(u, p):
                    copy.start()

    for n in range(max(chips - 1, PARTS)):
        if n < PARTS:
            relay(n)
        if n < chips - 1:
            pair_sum(n + 1)

    def add(coded_ref, scales_ref, s, at=None):
        for t in range(tpd):
            words = pl.ds(t * tile_dim, tile_dim)
            scaled = (pick[:, words] * scales_ref[(s if at is None else at) * tpd + t]).astype(jnp.bfloat16)
            high, low = split(coded_ref[s, words, :])
            total[...] += (jnp.dot(scaled, high, preferred_element_type=jnp.float32)
                           + jnp.dot(scaled, low, preferred_element_type=jnp.float32))

    def row_arrival(s):
        remote(eq.at[0], rq.at[s], row_send.at[0], row_recv.at[s], (r, 2 * s + e)).wait_recv()
        remote(es.at[tiles_of(0)], rs.at[tiles_of(s)], rsc_send.at[0], rsc_recv.at[s], (r, 2 * s + e)).wait_recv()

    def col_arrival(s):
        for p in range(PARTS):
            remote(qcol_ref.at[0, rows_of(p)], cq.at[s, rows_of(p)], col_send.at[0, p], col_recv.at[s, p],
                   (s, c)).wait_recv()
        remote(scol_ref.at[pl.ds(0, tpd)], cs.at[pl.ds(s * tpd, tpd)], csc_send.at[0], csc_recv.at[s],
               (s, c)).wait_recv()

    @pl.when(used)
    def _():
        own_copy(k).wait()
        for copy in pair_copies(k):
            copy.wait_recv()
        add(oq, srow_ref, k, c)
        add(pq, ps, k)

    for j in range(1, chips):
        s = lax.rem(k - j + chips, chips)

        @pl.when(s >= r * ratio // 2)
        def _(s=s):
            row_arrival(s)
            add(rq, rs, s)

    for d in range(n_row):
        @pl.when(r - d >= 0)
        def _(d=d):
            if d == 0:
                mine = c == (r * ratio + c // n_row)

                @pl.when(mine)
                def _():
                    for copy in col_here(c % n_row):
                        copy.wait()

                @pl.when(jnp.logical_not(mine))
                def _():
                    col_arrival(r)
            else:
                col_arrival(r - d)
            add(cq, cs, r - d)

    coded, scale = encode(total[...])
    qa[...] = coded.reshape(devices, pad, rank)
    lane = lax.broadcasted_iota(jnp.int32, (packed, 128), 1)
    within = lax.broadcasted_iota(jnp.int32, (packed, 128), 0) % pad
    spread = jnp.where(lane == within, scale, 0.0) + jnp.where(lane == within + 64, slot_sub, 0.0)
    meta[...] = jnp.broadcast_to(
        jnp.sum(spread.reshape(devices, pad, 128), axis=1, keepdims=True), meta.shape)

    def out_copies(d):
        to = lax.rem(me + d, devices)
        device = (to // n_col, to % n_col)
        return (
            remote(qa.at[to], ra.at[me], a_send.at[d], a_recv.at[me], device),
            remote(meta.at[to], rm.at[me], m_send.at[d], m_recv.at[me], device),
        )

    @pl.loop(1, devices)
    def _(d):
        for copy in out_copies(d):
            copy.start()
    here = (
        pltpu.make_async_copy(qa.at[me], ra.at[me], local_sem.at[0]),
        pltpu.make_async_copy(meta.at[me], rm.at[me], local_sem.at[1]),
    )
    for copy in here:
        copy.start()
    for copy in here:
        copy.wait()

    @pl.when(used)
    def _():
        for i in range(n_row):
            @pl.when(col_relayed(i))
            def _(i=i):
                for p in range(PARTS):
                    for copy in relay_copies(i, p):
                        copy.wait_send()

            @pl.when(col_direct(i))
            def _(i=i):
                for p in range(PARTS):
                    for copy in col_copies(i, p):
                        copy.wait_send()
        for j in range(1, chips):
            for copy in row_copies(lax.rem(k + j, chips)):
                copy.wait_send()
        for m in range(chips):
            for copy in pair_copies(m):
                copy.wait_send()

    for u in range(n_row - 1, 0, -1):
        @pl.when(hops(u))
        def _(u=u):
            for p in range(PARTS):
                for copy in hop_copies(u, p):
                    copy.wait_send()

    @pl.loop(1, devices)
    def _(d):
        s = lax.rem(me - d + devices, devices)
        device = (s // n_col, s % n_col)
        remote(qa.at[0], ra.at[s], a_send.at[0], a_recv.at[s], device).wait_recv()
        remote(meta.at[0], rm.at[s], m_send.at[0], m_recv.at[s], device).wait_recv()

    got = jnp.max(rm[...], axis=1)
    take = lax.broadcasted_iota(jnp.int32, (128, packed), 0)
    at = lax.broadcasted_iota(jnp.int32, (128, packed), 1) % pad
    mine = (lax.broadcasted_iota(jnp.int32, (devices, packed), 0)
            == lax.broadcasted_iota(jnp.int32, (devices, packed), 1) // pad)

    def lanes(offset):
        full = jnp.dot(got, (take == at + offset).astype(jnp.float32), precision=HIGHEST,
                       preferred_element_type=jnp.float32)
        return jnp.sum(jnp.where(mine, full, 0.0), axis=0, keepdims=True)

    scale_lane = lanes(0)
    slot_lane = jnp.round(lanes(64)).astype(jnp.int32)
    put = jnp.where(lax.broadcasted_iota(jnp.int32, (own, packed), 0) == slot_lane, scale_lane, 0.0).astype(jnp.bfloat16)
    high, low = split(ra[...].reshape(packed, rank))
    placed = (jnp.dot(put, high, preferred_element_type=jnp.float32)
              + jnp.dot(put, low, preferred_element_type=jnp.float32))
    out_ref[...] = jnp.dot(placed, ginv_ref[...], precision=HIGHEST, preferred_element_type=jnp.float32)

    @pl.loop(1, devices)
    def _(d):
        for copy in out_copies(d):
            copy.wait_send()


def per_device(n_row, n_col, tiles, tile_coord, tile_count, factors, owner, gram_inverse):
    own, rank = factors.shape
    tile_dim = tiles.shape[-1]
    slots = tiles.shape[2]
    devices = n_row * n_col
    row_tiles = own * n_col // tile_dim
    col_tiles = own * n_row // tile_dim
    tpd = own // tile_dim
    r = lax.axis_index("row")
    c = lax.axis_index("col")
    dma = pltpu.SemaphoreType.DMA

    panel = pl.pallas_call(
        functools.partial(gather_kernel, n_row, n_col),
        out_shape=jax.ShapeDtypeStruct((n_col + n_row, own, rank), factors.dtype),
        in_specs=[ANY],
        out_specs=ANY,
        scratch_shapes=[
            dma((n_col // 2,)), dma((n_col // 2,)), dma, dma((n_row,)),
            dma((n_col,)), dma((n_row,)), dma,
        ],
        compiler_params=pltpu.CompilerParams(collective_id=0, has_side_effects=True),
        name="gather",
    )(factors)

    per_step = 8
    steps = slots // per_step
    count = tile_count[0, 0]
    ratio = n_col // n_row
    first = jnp.where(r == c // ratio, (c % ratio) * col_tiles, row_tiles)
    numbers = jnp.stack([count, r * row_tiles, c * col_tiles, first]).astype(jnp.int32)
    whole = lambda *shape: pl.BlockSpec(shape, lambda g, a, b: (0,) * len(shape))
    qrow, qcol, srow, scol = pl.pallas_call(
        functools.partial(tile_kernel, per_step),
        out_shape=(
            jax.ShapeDtypeStruct((row_tiles, tile_dim, rank), jnp.int16),
            jax.ShapeDtypeStruct((col_tiles, tile_dim, rank), jnp.int16),
            jax.ShapeDtypeStruct((row_tiles, 1, tile_dim), jnp.float32),
            jax.ShapeDtypeStruct((col_tiles, 1, tile_dim), jnp.float32),
        ),
        grid_spec=pltpu.PrefetchScalarGridSpec(
            num_scalar_prefetch=2,
            grid=(steps,),
            in_specs=[
                pl.BlockSpec(
                    (per_step, tile_dim, tile_dim),
                    lambda g, a, b: (jnp.minimum(g, jnp.maximum(b[0] - 1, 0) // per_step), 0, 0),
                ),
                whole(row_tiles + col_tiles, tile_dim, rank),
            ],
            out_specs=(
                whole(row_tiles, tile_dim, rank),
                whole(col_tiles, tile_dim, rank),
                whole(row_tiles, 1, tile_dim),
                whole(col_tiles, 1, tile_dim),
            ),
            scratch_shapes=[
                pltpu.VMEM((row_tiles + 1, tile_dim, rank), jnp.float32),
                pltpu.VMEM((col_tiles + 1, tile_dim, rank), jnp.float32),
            ],
        ),
        compiler_params=pltpu.CompilerParams(vmem_limit_bytes=56 * MIB),
        name="tile_pass",
    )(
        tile_coord.reshape(-1), numbers, tiles.reshape(slots, tile_dim, tile_dim),
        panel.reshape(row_tiles + col_tiles, tile_dim, rank),
    )

    share = own // devices
    chips = n_col // 2
    pad = -(-share // 16) * 16
    packed = devices * pad
    return pl.pallas_call(
        functools.partial(solve_kernel, n_row, n_col, pad, tile_dim),
        out_shape=jax.ShapeDtypeStruct((own, rank), jnp.float32),
        in_specs=[ANY, ANY, VMEM, ANY, VMEM, VMEM, VMEM],
        out_specs=VMEM,
        scratch_shapes=[
            pltpu.VMEM((chips, own, rank), jnp.int16),
            pltpu.VMEM((chips * tpd, 1, tile_dim), jnp.float32),
            pltpu.VMEM((chips, own, rank), jnp.int16),
            pltpu.VMEM((chips, own, rank), jnp.int16),
            pltpu.VMEM((chips * tpd, 1, tile_dim), jnp.float32),
            pltpu.VMEM((chips, own, rank), jnp.int16),
            pltpu.VMEM((chips * tpd, 1, tile_dim), jnp.float32),
            pltpu.VMEM((n_row, own, rank), jnp.int16),
            pltpu.VMEM((n_row * tpd, 1, tile_dim), jnp.float32),
            pltpu.VMEM((n_row, own, rank), jnp.int16),
            pltpu.VMEM((n_row * tpd, 1, tile_dim), jnp.float32),
            pltpu.VMEM((packed, own), jnp.float32),
            pltpu.VMEM((packed, rank), jnp.float32),
            pltpu.VMEM((devices, pad, rank), jnp.int16),
            pltpu.VMEM((devices, 8, 128), jnp.float32),
            pltpu.VMEM((devices, pad, rank), jnp.int16),
            pltpu.VMEM((devices, 8, 128), jnp.float32),
            dma((chips,)), dma((chips,)), dma((chips,)), dma((chips,)), dma((chips,)),
            dma((chips,)), dma((chips,)), dma((n_row, PARTS)), dma((n_row,)),
            dma((chips,)), dma((chips,)), dma((n_row, PARTS)), dma((n_row,)),
            dma((n_row, PARTS)), dma((n_row,)), dma((n_row, PARTS)), dma((n_row,)),
            dma((devices,)), dma((devices,)), dma((devices,)), dma((devices,)), dma((2,)),
        ],
        compiler_params=pltpu.CompilerParams(
            collective_id=1, has_side_effects=True, vmem_limit_bytes=60 * MIB),
        name="solve",
    )(
        qrow.reshape(n_col, own, rank), qcol.reshape(n_row, own, rank), srow, scol,
        owner.reshape(1, own), owner.reshape(own, 1), gram_inverse,
    )


def solution(mesh):
    in_specs = (
        P("row", "col", None, None, None),
        P("row", "col", None, None),
        P("row", "col"),
        P(("row", "col"), None),
        P(("row", "col")),
        P(),
    )
    out_specs = P(("row", "col"), None)
    return jax.shard_map(
        functools.partial(per_device, mesh.shape["row"], mesh.shape["col"]),
        mesh=mesh, in_specs=in_specs, out_specs=out_specs, check_vma=False,
    )
```
